32 devices in a mesh: dp: 16 (over z, x, core), mp: 2 (over y).
Axes of the slice: x: 2, y: 2, z: 4, core: 2. Of those that a mesh axis runs over, the one named last changes fastest.
Arguments:
- normed_input_rows: bfloat16 [6144, 8192], P('dp', 'mp'), may hold values from -6 to 6
- frozen_queries: bfloat16 [6144, 8192], P('dp', 'mp'), may hold values from -6 to 6
- frozen_keys: bfloat16 [6144, 1024], P('dp', 'mp'), may hold values from -6 to 6
- frozen_values: bfloat16 [6144, 1024], P('dp', 'mp'), may hold values from -6 to 6
- attention_output_gradient: bfloat16 [6144, 8192], P('dp', 'mp'), may hold values from -1.1953125 to 1.1953125
- adapter_down_weight: float32 [64, 8192, 192], P(None, ('mp', 'dp')), may hold values from -0.0625 to 0.0625
- adapter_up_query: float32 [64, 64, 8192], P(None, 'dp', 'mp'), may hold values from -0.75 to 0.75
- adapter_up_key_value: float32 [64, 64, 8, 256], P(None, 'dp', 'mp'), may hold values from -0.75 to 0.75
- document_numbers: int32 [6144], P('dp'), may hold values from 0 to 383, as said below
- block_tenant_slot: int32 [48], P('dp'), may hold values from 0 to 1, as said below
- shard_tenant_table: int32 [16, 2], replicated, may hold values from 0 to 63, as said below
Outputs:
- grad_down: float32 [64, 8192, 192], P(None, ('mp', 'dp'))
- grad_upq: float32 [64, 64, 8192], P(None, 'dp', 'mp')
- grad_upkv: float32 [64, 64, 8, 256], P(None, 'dp', 'mp')
The draws below stay inside these ranges and needn't reach their ends.
Inputs may be any that keep to these rules, and one draw needn't show every extreme that they name: `document_numbers`: document numbers never fall along the rows; a document starts only at a multiple of 16 rows, always at the first row of each index of dp, at the last 16 rows of all, and wherever the slot of a block changes; a document's number is its first row divided by 16. `block_tenant_slot`: the 3 blocks of each index of dp name slots in an order that never falls, and every one of the 2 slots is named. `shard_tenant_table`: each row holds 2 distinct tenants.
All inputs are finite; a program needn't handle non-finite values.
Results may differ from the reference program's by a relative error of at most 0.012.
The reference program's roundings to bfloat16 on the way count: a program that leaves them out, or rounds other values in their place, can miss the bound.
Values sent between devices are 32-bit elements; how exact they have to be, the bound alone decides.
No kernel may reach another device: no remote copies, remote signals or barrier semaphores. Data moves between devices by JAX's collectives and lax.ppermute only.
A program may use at most 192 MiB of HBM per device.

```python
import jax
import jax.numpy as jnp
from jax import lax

MODEL_WIDTH = 8192
QUERY_HEADS = 64
KEY_VALUE_HEADS = 8
HEAD_WIDTH = 128
ADAPTER_RANK = 64
TENANT_COUNT = 64
TENANT_BLOCK = 128
SLOTS = 2
TOKENS_PER_SHARD = 384
TOKEN_COUNT = 6144
N_DP = 16


def base_fields(key):
    query_noise = jax.random.normal(jax.random.fold_in(key, 11), (TOKEN_COUNT, QUERY_HEADS * HEAD_WIDTH), jnp.float32)
    key_perturbation = jax.random.normal(jax.random.fold_in(key, 12), (TOKEN_COUNT, KEY_VALUE_HEADS * HEAD_WIDTH), jnp.float32)
    query_noise = jnp.clip(query_noise, -6.0, 6.0)
    key_perturbation = jnp.clip(key_perturbation, -6.0, 6.0)
    return (query_noise, key_perturbation)


def draw_frozen_queries(key, part):
    return base_fields(key)[0].astype(jnp.bfloat16)


def draw_frozen_keys(key, part):
    return base_fields(key)[1].astype(jnp.bfloat16)


def tenant_layout(key):
    per_device = TOKENS_PER_SHARD // TENANT_BLOCK
    dev_keys = jax.random.split(jax.random.fold_in(key, 21), N_DP)
    order_ranks = jax.vmap(lambda single: jax.random.permutation(single, per_device - 1))(dev_keys)
    cut_flags = (order_ranks < SLOTS - 1).astype(jnp.int32)
    slot_rows = jnp.concatenate([jnp.zeros((N_DP, 1), jnp.int32), jnp.cumsum(cut_flags, axis=1).astype(jnp.int32)], axis=1)
    group_total = TOKENS_PER_SHARD // 16
    group_index = jnp.arange(group_total, dtype=jnp.int32)
    fresh_start = jax.random.randint(jax.random.fold_in(key, 22), (N_DP, group_total), 0, 4) == 0
    change = jnp.concatenate([jnp.zeros((N_DP, 1), bool), slot_rows[:, 1:] != slot_rows[:, :-1]], axis=1)
    at_block = group_index % (TENANT_BLOCK // 16) == 0
    change_groups = change[:, group_index // (TENANT_BLOCK // 16)] & at_block[None, :]
    start_flags = fresh_start | (group_index == 0)[None, :] | change_groups
    flat_flags = start_flags.reshape(-1)
    every_group = jnp.arange(N_DP * group_total, dtype=jnp.int32)
    flat_flags = flat_flags | (every_group == N_DP * group_total - 1)
    doc_groups = lax.cummax(jnp.where(flat_flags, every_group, 0).astype(jnp.int32), axis=0)
    return (slot_rows.reshape(-1), jnp.repeat(doc_groups, 16).astype(jnp.int32))


def draw_document_numbers(key, part):
    return tenant_layout(key)[1]


def draw_block_tenant_slot(key, part):
    return tenant_layout(key)[0]


def draw_shard_tenant_table(key, part):
    widest = (TENANT_COUNT - 1) // (SLOTS - 1)
    first_draw = jax.random.randint(jax.random.fold_in(key, 31), (N_DP,), 0, TENANT_COUNT)
    second_draw = jax.random.randint(jax.random.fold_in(key, 32), (N_DP,), 0, TENANT_COUNT)
    base_ids = jnp.minimum(first_draw, second_draw)
    stride = jax.random.randint(jax.random.fold_in(key, 33), (N_DP,), 1, widest + 1)
    row_index = jnp.arange(N_DP, dtype=jnp.int32)
    low_row = jax.random.randint(jax.random.fold_in(key, 34), (), 0, N_DP)
    high_row = (low_row + 1) % N_DP
    base_ids = jnp.where(row_index == low_row, 0, jnp.where(row_index == high_row, TENANT_COUNT - 1 - (SLOTS - 1) * widest, base_ids))
    stride = jnp.where((row_index == low_row) | (row_index == high_row), widest, stride)
    tenant_rows = (base_ids[:, None] + stride[:, None] * jnp.arange(SLOTS, dtype=jnp.int32)[None, :]) % TENANT_COUNT
    return tenant_rows.astype(jnp.int32)


def shard_levels(key, dims, cuts, least, top_value):
    level = 1.0
    for dim, blocks in cuts:
        steps = jax.random.uniform(jax.random.fold_in(jax.random.fold_in(key, 6), dim), (blocks,), jnp.float32, least / len(cuts), top_value / len(cuts))
        level = level * jnp.repeat(jnp.exp(steps), dims[dim] // blocks).reshape((-1,) + (1,) * (len(dims) - 1 - dim))
    return level


def scatter_about(own_key, shape, spread, limit, cuts=(), held_as=jnp.bfloat16):
    gain = shard_levels(own_key, shape, cuts, -0.22, 0.18) if cuts else 1.0
    result = jax.random.normal(own_key, shape, jnp.float32) * spread * gain
    return jnp.minimum(jnp.maximum(result, -limit), limit).astype(held_as)


def setup_inputs(seed: int = 0) -> dict:
    key_of = jax.random.split(jax.random.key(seed), 12)
    normed_input_rows = scatter_about(key_of[0], (TOKEN_COUNT, MODEL_WIDTH), 1.0, 6.0, ((0, 16), (1, 2)))
    frozen_queries = draw_frozen_queries(jax.random.fold_in(key_of[11], 71), 0)
    frozen_keys = draw_frozen_keys(jax.random.fold_in(key_of[11], 71), 0)
    frozen_values = scatter_about(key_of[3], (TOKEN_COUNT, KEY_VALUE_HEADS * HEAD_WIDTH), 1.0, 6.0, ((0, 16), (1, 2)))
    attention_output_gradient = scatter_about(key_of[4], (TOKEN_COUNT, QUERY_HEADS * HEAD_WIDTH), 0.2, 1.1953125, ((0, 16), (1, 2)))
    adapter_down_weight = scatter_about(key_of[5], (TENANT_COUNT, MODEL_WIDTH, 3 * ADAPTER_RANK), MODEL_WIDTH ** -0.5, 0.0625, ((1, 32),), jnp.float32)
    adapter_up_query = scatter_about(key_of[6], (TENANT_COUNT, ADAPTER_RANK, QUERY_HEADS * HEAD_WIDTH), ADAPTER_RANK ** -0.5, 0.75, ((1, 16), (2, 2)), jnp.float32)
    adapter_up_key_value = scatter_about(key_of[7], (TENANT_COUNT, ADAPTER_RANK, KEY_VALUE_HEADS, 2 * HEAD_WIDTH), ADAPTER_RANK ** -0.5, 0.75, ((1, 16), (2, 2)), jnp.float32)
    document_numbers = draw_document_numbers(jax.random.fold_in(key_of[11], 71), 0)
    block_tenant_slot = draw_block_tenant_slot(jax.random.fold_in(key_of[11], 71), 0)
    shard_tenant_table = draw_shard_tenant_table(jax.random.fold_in(key_of[11], 71), 0)
    return {"normed_input_rows": normed_input_rows, "frozen_queries": frozen_queries, "frozen_keys": frozen_keys, "frozen_values": frozen_values, "attention_output_gradient": attention_output_gradient, "adapter_down_weight": adapter_down_weight, "adapter_up_query": adapter_up_query, "adapter_up_key_value": adapter_up_key_value, "document_numbers": document_numbers, "block_tenant_slot": block_tenant_slot, "shard_tenant_table": shard_tenant_table}


ADAPTER_SCALE = 0.5
MASKED = -1e30
PRECISION_HIGH = lax.Precision.HIGHEST


def attention_grads(query_row_block, key_row_block, value_row_block, upstream, doc_row):
    row_total = query_row_block.shape[0]
    kv_heads = key_row_block.shape[1]
    groups = query_row_block.shape[1] // kv_heads
    head_size = query_row_block.shape[2]
    query_g = query_row_block.reshape(row_total, kv_heads, groups, head_size).astype(jnp.float32)
    key_f = key_row_block.astype(jnp.float32)
    value_f = value_row_block.astype(jnp.float32)
    upstream_g = upstream.reshape(row_total, kv_heads, groups, head_size).astype(jnp.float32)
    inverse = 1.0 / (head_size ** 0.5)
    scores = jnp.einsum("qkgd,jkd->kgqj", query_g, key_f, precision=PRECISION_HIGH) * inverse
    position = jnp.arange(row_total, dtype=jnp.int32)
    allowed = (doc_row[:, None] == doc_row[None, :]) & (position[:, None] >= position[None, :])
    scores = jnp.where(allowed, scores, MASKED)
    row_top = jnp.max(scores, axis=-1, keepdims=True)
    weights = jnp.exp(scores - row_top)
    attn_probs = weights / jnp.sum(weights, axis=-1, keepdims=True)
    probs_low = lax.optimization_barrier(attn_probs.astype(jnp.bfloat16)).astype(jnp.float32)
    grad_probs = jnp.einsum("qkgd,jkd->kgqj", upstream_g, value_f, precision=PRECISION_HIGH)
    row_inner = jnp.sum(attn_probs * grad_probs, axis=-1, keepdims=True)
    grad_scores = (attn_probs * (grad_probs - row_inner) * inverse).astype(jnp.bfloat16)
    grad_scores = lax.optimization_barrier(grad_scores).astype(jnp.float32)
    grad_query = jnp.einsum("kgqj,jkd->qkgd", grad_scores, key_f, precision=PRECISION_HIGH).reshape(row_total, -1)
    key_gradient = jnp.einsum("kgqj,qkgd->jkd", grad_scores, query_g, precision=PRECISION_HIGH).reshape(row_total, -1)
    value_gradient = jnp.einsum("kgqj,qkgd->jkd", probs_low, upstream_g, precision=PRECISION_HIGH).reshape(row_total, -1)
    return grad_query, key_gradient, value_gradient


def reference(normed_input_rows, frozen_queries, frozen_keys, frozen_values, attention_output_gradient, adapter_down_weight, adapter_up_query, adapter_up_key_value, document_numbers, block_tenant_slot, shard_tenant_table):
    total_blocks = TOKEN_COUNT // TENANT_BLOCK
    per_device = TOKENS_PER_SHARD // TENANT_BLOCK
    device_of = (jnp.arange(total_blocks, dtype=jnp.int32) // per_device).astype(jnp.int32)
    owner = shard_tenant_table[device_of, block_tenant_slot].astype(jnp.int32)
    row_blocks = normed_input_rows.reshape(total_blocks, TENANT_BLOCK, MODEL_WIDTH)

    def panels_of(tenant_index):
        query_adapter_panel = adapter_up_query[tenant_index]
        key_value_adapter_panel = adapter_up_key_value[tenant_index]
        key_adapter_panel = key_value_adapter_panel[:, :, :HEAD_WIDTH].reshape(ADAPTER_RANK, KEY_VALUE_HEADS * HEAD_WIDTH)
        value_adapter_panel = key_value_adapter_panel[:, :, HEAD_WIDTH:].reshape(ADAPTER_RANK, KEY_VALUE_HEADS * HEAD_WIDTH)
        return query_adapter_panel, key_adapter_panel, value_adapter_panel

    def forward_block(block_item):
        incoming_rows, tenant_index = block_item
        down_projected_rows = jnp.dot(incoming_rows.astype(jnp.float32), adapter_down_weight[tenant_index], precision=PRECISION_HIGH)
        query_adapter_panel, key_adapter_panel, value_adapter_panel = panels_of(tenant_index)
        query_addition = jnp.dot(down_projected_rows[:, :ADAPTER_RANK], query_adapter_panel, precision=PRECISION_HIGH)
        key_addition = jnp.dot(down_projected_rows[:, ADAPTER_RANK:2 * ADAPTER_RANK], key_adapter_panel, precision=PRECISION_HIGH)
        value_addition = jnp.dot(down_projected_rows[:, 2 * ADAPTER_RANK:], value_adapter_panel, precision=PRECISION_HIGH)
        return down_projected_rows, query_addition, key_addition, value_addition

    lowrank, query_addition, key_addition, value_addition = lax.map(forward_block, (row_blocks, owner))
    query_row_block = (frozen_queries.astype(jnp.float32) + ADAPTER_SCALE * query_addition.reshape(TOKEN_COUNT, QUERY_HEADS * HEAD_WIDTH)).astype(jnp.bfloat16)
    key_row_block = (frozen_keys.astype(jnp.float32) + ADAPTER_SCALE * key_addition.reshape(TOKEN_COUNT, KEY_VALUE_HEADS * HEAD_WIDTH)).astype(jnp.bfloat16)
    value_row_block = (frozen_values.astype(jnp.float32) + ADAPTER_SCALE * value_addition.reshape(TOKEN_COUNT, KEY_VALUE_HEADS * HEAD_WIDTH)).astype(jnp.bfloat16)

    def device_item(dev_item):
        q_dev, k_dev, v_dev, o_dev, doc_dev = dev_item
        return attention_grads(q_dev, k_dev, v_dev, o_dev, doc_dev)

    grad_query, key_gradient, value_gradient = lax.map(device_item, (
        query_row_block.reshape(N_DP, TOKENS_PER_SHARD, QUERY_HEADS, HEAD_WIDTH),
        key_row_block.reshape(N_DP, TOKENS_PER_SHARD, KEY_VALUE_HEADS, HEAD_WIDTH),
        value_row_block.reshape(N_DP, TOKENS_PER_SHARD, KEY_VALUE_HEADS, HEAD_WIDTH),
        attention_output_gradient.reshape(N_DP, TOKENS_PER_SHARD, QUERY_HEADS, HEAD_WIDTH),
        document_numbers.reshape(N_DP, TOKENS_PER_SHARD)))
    grad_query = grad_query.reshape(total_blocks, TENANT_BLOCK, QUERY_HEADS * HEAD_WIDTH)
    key_gradient = key_gradient.reshape(total_blocks, TENANT_BLOCK, KEY_VALUE_HEADS * HEAD_WIDTH)
    value_gradient = value_gradient.reshape(total_blocks, TENANT_BLOCK, KEY_VALUE_HEADS * HEAD_WIDTH)

    def backward_block(carry, block_item):
        acc_down, acc_q, acc_kv = carry
        incoming_rows, tenant_index, down_projected_rows, query_gradient_rows, key_gradient_rows, value_gradient_rows = block_item
        query_adapter_panel, key_adapter_panel, value_adapter_panel = panels_of(tenant_index)
        lowrank_gradient = ADAPTER_SCALE * jnp.concatenate([
            jnp.dot(query_gradient_rows, query_adapter_panel.T, precision=PRECISION_HIGH),
            jnp.dot(key_gradient_rows, key_adapter_panel.T, precision=PRECISION_HIGH),
            jnp.dot(value_gradient_rows, value_adapter_panel.T, precision=PRECISION_HIGH)], axis=-1)
        term_down = jnp.dot(incoming_rows.astype(jnp.float32).T, lowrank_gradient, precision=PRECISION_HIGH)
        query_term = ADAPTER_SCALE * jnp.dot(down_projected_rows[:, :ADAPTER_RANK].T, query_gradient_rows, precision=PRECISION_HIGH)
        key_term = (ADAPTER_SCALE * jnp.dot(down_projected_rows[:, ADAPTER_RANK:2 * ADAPTER_RANK].T, key_gradient_rows, precision=PRECISION_HIGH)).reshape(ADAPTER_RANK, KEY_VALUE_HEADS, HEAD_WIDTH)
        value_term = (ADAPTER_SCALE * jnp.dot(down_projected_rows[:, 2 * ADAPTER_RANK:].T, value_gradient_rows, precision=PRECISION_HIGH)).reshape(ADAPTER_RANK, KEY_VALUE_HEADS, HEAD_WIDTH)
        term_kv = jnp.concatenate([key_term, value_term], axis=-1)
        return (acc_down.at[tenant_index].add(term_down), acc_q.at[tenant_index].add(query_term), acc_kv.at[tenant_index].add(term_kv)), None

    start = (jnp.zeros((TENANT_COUNT, MODEL_WIDTH, 3 * ADAPTER_RANK), jnp.float32),
             jnp.zeros((TENANT_COUNT, ADAPTER_RANK, QUERY_HEADS * HEAD_WIDTH), jnp.float32),
             jnp.zeros((TENANT_COUNT, ADAPTER_RANK, KEY_VALUE_HEADS, 2 * HEAD_WIDTH), jnp.float32))
    (grad_down, grad_upq, grad_upkv), _ = lax.scan(backward_block, start, (row_blocks, owner, lowrank, grad_query, key_gradient, value_gradient))
    return grad_down, grad_upq, grad_upkv
```

```python
import functools

import jax
import jax.numpy as jnp
from jax import lax
from jax.experimental import pallas as pl
from jax.experimental.pallas import tpu as pltpu
from jax.sharding import PartitionSpec as P

ADAPTER_SCALE = 0.5
MASKED = -1e30
BF16, F32 = jnp.bfloat16, jnp.float32
VMEM_LIMIT = 56 * 1024 * 1024
NN = (((1,), (0,)), ((), ()))
NT = (((1,), (1,)), ((), ()))
TN = (((0,), (0,)), ((), ()))
HEADS_PER_CALL = 4


def split2(a):
    high = a.astype(BF16)
    return high, (a - high.astype(F32)).astype(BF16)


def mm(a, b, dims=NN):
    return lax.dot_general(a, b, dims, preferred_element_type=F32)


def mm3(a, b, dims=NN):
    (ah, al), (bh, bl) = a, b
    return mm(ah, bh, dims) + mm(ah, bl, dims) + mm(al, bh, dims)


def bit_reverse(value, bits):
    out = jnp.zeros_like(value)
    for k in range(bits):
        out = out | (((value >> k) & 1) << (bits - 1 - k))
    return out


def swap(a, axis, size, bit):
    return lax.ppermute(a, axis, [(i, i ^ bit) for i in range(size)])


def sum_over(a, axis, size):
    bit = 1
    while bit < size:
        a = a + swap(a, axis, size, bit)
        bit *= 2
    return a


def scatter_sum(part, axis, size):
    bit = 1
    while bit < size:
        half = part.shape[0] // 2
        part = part[:half] + swap(part[half:], axis, size, bit)
        bit *= 2
    return part[0]


def gather_halves(a, axis, size):
    a = a[None]
    bit = size // 2
    while bit > 1:
        a = jnp.concatenate([a, swap(a, axis, size, bit)], axis=0)
        bit //= 2
    return a, swap(a, axis, size, 1)


def by_tenant(owners, tenants):
    count = owners.shape[0]
    index = jnp.arange(count, dtype=jnp.int32)
    ahead = (owners[None, :] < owners[:, None]) | (
        (owners[None, :] == owners[:, None]) & (index[None, :] < index[:, None])
    )
    place = jnp.sum(ahead.astype(jnp.int32), axis=1)
    order = jnp.sum(
        jnp.where(place[None, :] == index[:, None], index[None, :], 0), axis=1
    )
    edge = jnp.arange(tenants + 1, dtype=jnp.int32)
    first = jnp.sum((owners[None, :] < edge[:, None]).astype(jnp.int32), axis=1)
    return order.astype(jnp.int32), first.astype(jnp.int32)


def down_kernel(source_ref, tenant_ref, x_ref, w_ref, out_ref):
    x = x_ref[0].astype(BF16)
    high, low = split2(w_ref[0])
    out_ref[0] = mm(high, x, NT) + mm(low, x, NT)


def down_partial(x, weights, source, tenant):
    n, rows, width = x.shape
    rank = weights.shape[1]
    return pl.pallas_call(
        down_kernel,
        grid_spec=pltpu.PrefetchScalarGridSpec(
            num_scalar_prefetch=2,
            grid=(n,),
            in_specs=[
                pl.BlockSpec((1, rows, width), lambda p, s, t: (s[p], 0, 0)),
                pl.BlockSpec((1, rank, width), lambda p, s, t: (t[p], 0, 0)),
            ],
            out_specs=pl.BlockSpec((1, rank, rows), lambda p, s, t: (p, 0, 0)),
        ),
        out_shape=jax.ShapeDtypeStruct((n, rank, rows), F32),
        compiler_params=pltpu.CompilerParams(vmem_limit_bytes=VMEM_LIMIT),
        name="down_partial",
    )(source, tenant, x, weights)


def attention_kernel(
    groups,
    blocks,
    slots,
    fq_ref,
    fk_ref,
    fv_ref,
    up_ref,
    *rest,
):
    low_refs = rest[:blocks]
    (
        panel_ref,
        slot_ref,
        doc_row_ref,
        doc_col_ref,
        du_ref,
        g_ref,
        bias,
        low_t,
        lct_h,
        lct_l,
        lc_h,
        lc_l,
        panel,
        du,
        q_s,
        dq_s,
        dk_t,
        dv_t,
    ) = rest[blocks:]
    step = pl.program_id(0)
    rows, head = fk_ref.shape
    block = rows // blocks
    owners, _, piece, _ = panel_ref.shape
    rank = owners * piece
    wide = groups * head
    inverse = 1.0 / head**0.5
    slot = slot_ref[...]

    @pl.when(step == 0)
    def _():
        row = lax.broadcasted_iota(jnp.int32, (rows, rows), 0)
        col = lax.broadcasted_iota(jnp.int32, (rows, rows), 1)
        joined = (doc_row_ref[...] == doc_col_ref[...]) & (row >= col)
        bias[...] = jnp.where(joined, 0.0, MASKED)
        for b in range(blocks):
            low_t[:, b * block : (b + 1) * block] = low_refs[b][...]
        for part in range(3):
            low = low_t[part * rank : (part + 1) * rank, :] * ADAPTER_SCALE
            for s in range(slots):
                mine = jnp.where(slot == s, low, 0.0)
                span = slice(s * rank, (s + 1) * rank)
                high, rest_ = split2(mine)
                lct_h[part, span, :] = high
                lct_l[part, span, :] = rest_
            both = jnp.concatenate(
                [jnp.where(slot == s, low, 0.0) for s in range(slots)], axis=0
            ).T
            high, rest_ = split2(both)
            lc_h[part] = high
            lc_l[part] = rest_
        g_ref[...] = jnp.zeros_like(g_ref)

    for w in range(owners):
        for s in range(slots):
            start = s * rank + w * piece
            panel[start : start + piece, :] = panel_ref[w, s]
    u_q = split2(panel[:, :wide])
    u_k = split2(panel[:, wide : wide + head])
    u_v = split2(panel[:, wide + head :])
    k = (fk_ref[...].astype(F32) + mm3((lc_h[1], lc_l[1]), u_k)).astype(BF16)
    v = (fv_ref[...].astype(F32) + mm3((lc_h[2], lc_l[2]), u_v)).astype(BF16)
    q_s[...] = (fq_ref[...].astype(F32) + mm3((lc_h[0], lc_l[0]), u_q)).astype(BF16)
    dk_t[...] = jnp.zeros_like(dk_t)
    dv_t[...] = jnp.zeros_like(dv_t)

    for b in range(blocks):
        here = slice(b * block, (b + 1) * block)
        reach = (b + 1) * block
        kk, vv = k[:reach], v[:reach]
        mask = bias[here, :reach]
        for h in range(groups):
            lanes = slice(h * head, (h + 1) * head)
            q = q_s[here, lanes]
            up = up_ref[here, lanes]
            scores = mm(q, kk, NT) * inverse + mask
            top = jnp.max(scores, axis=-1, keepdims=True)
            weights = jnp.exp(scores - top)
            total = jnp.sum(weights, axis=-1, keepdims=True)
            probs = weights * (1.0 / total)
            grad_probs = mm(up, vv, NT)
            inner = jnp.sum(probs * grad_probs, axis=-1, keepdims=True)
            grad_scores = (probs * (grad_probs - inner) * inverse).astype(BF16)
            dq_s[here, lanes] = mm(grad_scores, kk)
            dk_t[:, :reach] += mm(q, grad_scores, TN)
            dv_t[:, :reach] += mm(up, probs.astype(BF16), TN)

    dq = split2(dq_s[...])
    dk = split2(dk_t[...])
    dv = split2(dv_t[...])
    du[:, :wide] = mm3((lct_h[0], lct_l[0]), dq)
    du[:, wide : wide + head] = mm3((lct_h[1], lct_l[1]), dk, NT)
    du[:, wide + head :] = mm3((lct_h[2], lct_l[2]), dv, NT)
    for w in range(owners):
        for s in range(slots):
            start = s * rank + w * piece
            du_ref[w, s] = du[start : start + piece, :]
    for part, both in enumerate((mm3(u_q, dq, NT), mm3(u_k, dk), mm3(u_v, dv))):
        mine = jnp.zeros((rank, rows), F32)
        for s in range(slots):
            mine += jnp.where(slot == s, both[s * rank : (s + 1) * rank], 0.0)
        mine *= ADAPTER_SCALE
        for b in range(blocks):
            g_ref[b, part * rank : (part + 1) * rank, :] += mine[
                :, b * block : (b + 1) * block
            ]


def attention(fq, fk, fv, up, lows, panels, slot_rows, docs, head, first, heads):
    rows = fq.shape[0]
    blocks = len(lows)
    block = rows // blocks
    n, slots, piece, cols = panels.shape
    kv_heads = fk.shape[1] // head
    groups = fq.shape[1] // fk.shape[1]
    wide = groups * head
    per = wide + 2 * head
    rank = n * piece
    whole = lambda shape: pl.BlockSpec(shape, lambda g: (0,) * len(shape))
    spans = slots * rank
    return pl.pallas_call(
        functools.partial(attention_kernel, groups, blocks, slots),
        grid=(heads,),
        in_specs=[
            pl.BlockSpec((rows, wide), lambda g: (0, first + g)),
            pl.BlockSpec((rows, head), lambda g: (0, first + g)),
            pl.BlockSpec((rows, head), lambda g: (0, first + g)),
            pl.BlockSpec((rows, wide), lambda g: (0, first + g)),
        ]
        + [whole((3 * rank, block))] * blocks
        + [
            pl.BlockSpec((n, slots, piece, per), lambda g: (0, 0, 0, g)),
            whole((1, rows)),
            whole((1, rows)),
            whole((rows, 1)),
        ],
        out_specs=[
            pl.BlockSpec((n, slots, piece, per), lambda g: (0, 0, 0, g)),
            whole((blocks, 3 * rank, block)),
        ],
        out_shape=[
            jax.ShapeDtypeStruct((n, slots, piece, heads * per), F32),
            jax.ShapeDtypeStruct((blocks, 3 * rank, block), F32),
        ],
        scratch_shapes=[
            pltpu.VMEM((rows, rows), F32),
            pltpu.VMEM((3 * rank, rows), F32),
            pltpu.VMEM((3, spans, rows), BF16),
            pltpu.VMEM((3, spans, rows), BF16),
            pltpu.VMEM((3, rows, spans), BF16),
            pltpu.VMEM((3, rows, spans), BF16),
            pltpu.VMEM((spans, per), F32),
            pltpu.VMEM((spans, per), F32),
            pltpu.VMEM((rows, wide), BF16),
            pltpu.VMEM((rows, wide), F32),
            pltpu.VMEM((head, rows), F32),
            pltpu.VMEM((head, rows), F32),
        ],
        compiler_params=pltpu.CompilerParams(vmem_limit_bytes=VMEM_LIMIT),
        name="attention_grads",
    )(fq, fk, fv, up, *lows, panels, slot_rows, docs[None, :], docs[:, None])


def down_grad_kernel(blocks, per_step, order_ref, first_ref, source_ref, *refs):
    x_refs, (g0_ref, g1_ref, out_ref, x_all, g_ref, sems) = refs[:blocks], refs[blocks:]
    half = g0_ref.shape[0]
    step = pl.program_id(0)

    @pl.when(step == 0)
    def _():
        copies = [
            pltpu.make_async_copy(x_refs[b], x_all.at[b], sems.at[b]) for b in range(blocks)
        ] + [
            pltpu.make_async_copy(
                ref, g_ref.at[pl.ds(side * half, half)], sems.at[blocks + side]
            )
            for side, ref in enumerate((g0_ref, g1_ref))
        ]
        for copy in copies:
            copy.start()
        for copy in copies:
            copy.wait()

    for t in range(per_step):
        tenant = step * per_step + t
        out_ref[t] = jnp.zeros(out_ref.shape[1:], F32)

        def add(e, carry):
            item = order_ref[e]
            place = item // blocks
            b = item - place * blocks
            x = x_all[b, source_ref[place]].astype(BF16)
            high, low = split2(g_ref[place, b])
            out_ref[t] += mm(high, x) + mm(low, x)
            return carry

        lax.fori_loop(first_ref[tenant], first_ref[tenant + 1], add, 0)


def down_grad(xs, g, order, first, source, tenants):
    blocks = len(xs)
    n, rows, width = xs[0].shape
    rank = g[0].shape[2]
    per_step = 8
    return pl.pallas_call(
        functools.partial(down_grad_kernel, blocks, per_step),
        grid_spec=pltpu.PrefetchScalarGridSpec(
            num_scalar_prefetch=3,
            grid=(tenants // per_step,),
            in_specs=[pl.BlockSpec(memory_space=pl.ANY)] * (blocks + 2),
            out_specs=pl.BlockSpec((per_step, rank, width), lambda i, *_: (i, 0, 0)),
            scratch_shapes=[
                pltpu.VMEM((blocks, n, rows, width), F32),
                pltpu.VMEM((n,) + g[0].shape[1:], F32),
                pltpu.SemaphoreType.DMA((blocks + 2,)),
            ],
        ),
        out_shape=jax.ShapeDtypeStruct((tenants, rank, width), F32),
        compiler_params=pltpu.CompilerParams(vmem_limit_bytes=VMEM_LIMIT),
        name="down_grad",
    )(order, first, source, *xs, *g)


def up_grad_kernel(calls, per_step, kv_heads, head, order_ref, first_ref, *refs):
    in_refs, (q_ref, kv_ref) = refs[:calls], refs[calls:]
    step = pl.program_id(0)
    wide = q_ref.shape[2] // kv_heads
    per = wide + 2 * head
    heads = kv_heads // calls
    for t in range(per_step):
        tenant = step * per_step + t
        q_ref[t] = jnp.zeros(q_ref.shape[1:], F32)
        kv_ref[t] = jnp.zeros(kv_ref.shape[1:], F32)

        def add(e, carry):
            item = order_ref[e]
            for c in range(calls):
                for h in range(heads):
                    at = c * heads + h
                    q_ref[t, :, at * wide : (at + 1) * wide] += in_refs[c][
                        item, :, h * per : h * per + wide
                    ]
                    kv_ref[t, at] += in_refs[c][item, :, h * per + wide : (h + 1) * per]
            return carry

        lax.fori_loop(first_ref[tenant], first_ref[tenant + 1], add, 0)


def up_grad(dus, order, first, tenants, kv_heads, head):
    calls = len(dus)
    items, piece, cols = dus[0].shape
    per_step = 8
    wide = cols * calls // kv_heads - 2 * head
    return pl.pallas_call(
        functools.partial(up_grad_kernel, calls, per_step, kv_heads, head),
        grid_spec=pltpu.PrefetchScalarGridSpec(
            num_scalar_prefetch=2,
            grid=(tenants // per_step,),
            in_specs=[pl.BlockSpec((items, piece, cols), lambda i, *_: (0, 0, 0))] * calls,
            out_specs=[
                pl.BlockSpec((per_step, piece, kv_heads * wide), lambda i, *_: (i, 0, 0)),
                pl.BlockSpec((per_step, kv_heads, piece, 2 * head), lambda i, *_: (i, 0, 0, 0)),
            ],
        ),
        out_shape=[
            jax.ShapeDtypeStruct((tenants, piece, kv_heads * wide), F32),
            jax.ShapeDtypeStruct((tenants, kv_heads, piece, 2 * head), F32),
        ],
        compiler_params=pltpu.CompilerParams(vmem_limit_bytes=VMEM_LIMIT),
        name="up_grad",
    )(order, first, *dus)


def exchange(a):
    return lax.all_to_all(a, "dp", split_axis=0, concat_axis=0, tiled=True)


def on_device(
    dp_count,
    mp_count,
    normed_input_rows,
    frozen_queries,
    frozen_keys,
    frozen_values,
    attention_output_gradient,
    adapter_down_weight,
    adapter_up_query,
    adapter_up_key_value,
    document_numbers,
    block_tenant_slot,
    shard_tenant_table,
):
    rows = normed_input_rows.shape[0]
    blocks = block_tenant_slot.shape[0]
    block = rows // blocks
    tenants, width, ranks = adapter_down_weight.shape
    slots = shard_tenant_table.shape[1]
    piece = adapter_up_query.shape[1]
    kv_heads = adapter_up_key_value.shape[2]
    head = adapter_up_key_value.shape[3] // 2
    wide = adapter_up_query.shape[2] // kv_heads
    me = lax.axis_index("dp").astype(jnp.int32)

    xs = [
        exchange(
            normed_input_rows[b * block : (b + 1) * block]
            .reshape(block, dp_count, width)
            .transpose(1, 0, 2)
            .astype(F32)
        )
        for b in range(blocks)
    ]

    source = me ^ bit_reverse(
        jnp.arange(dp_count, dtype=jnp.int32), dp_count.bit_length() - 1
    )
    slots_all = jnp.concatenate(gather_halves(block_tenant_slot, "dp", dp_count), axis=0)
    owners = shard_tenant_table[source[:, None], slots_all]

    wanted = shard_tenant_table.reshape(-1)
    up_query = adapter_up_query[wanted].reshape(-1, piece, kv_heads, wide)
    up_key_value = adapter_up_key_value[wanted]
    wire = jnp.concatenate([up_query, up_key_value], axis=-1)
    heads = min(HEADS_PER_CALL, kv_heads)
    calls = kv_heads // heads
    per = wide + 2 * head
    panels = [
        exchange(
            wire[:, :, c * heads : (c + 1) * heads].reshape(-1, piece, heads * per)
        ).reshape(dp_count, slots, piece, heads * per)
        for c in range(calls)
    ]

    weights = jnp.swapaxes(adapter_down_weight, 1, 2)
    lows = []
    for b in range(blocks):
        part = down_partial(xs[b], weights, source, owners[:, b])
        lows.append(sum_over(scatter_sum(part, "dp", dp_count), "mp", mp_count))

    slot_rows = jnp.repeat(block_tenant_slot, block)[None, :]
    dus, g = [], None
    for c in range(calls):
        du, g_part = attention(
            frozen_queries,
            frozen_keys,
            frozen_values,
            attention_output_gradient,
            lows,
            panels[c],
            slot_rows,
            document_numbers,
            head,
            c * heads,
            heads,
        )
        dus.append(exchange(du.reshape(dp_count * slots, piece, heads * per)))
        g = g_part if g is None else g + g_part

    g_halves = gather_halves(sum_over(g, "mp", mp_count), "dp", dp_count)
    order, first = by_tenant(owners.reshape(-1), tenants)
    grad_down = down_grad(xs, g_halves, order, first, source, tenants)
    order, first = by_tenant(wanted, tenants)
    grad_upq, grad_upkv = up_grad(dus, order, first, tenants, kv_heads, head)
    return (
        jnp.swapaxes(grad_down, 1, 2),
        grad_upq,
        jnp.swapaxes(grad_upkv, 1, 2),
    )


def solution(mesh):
    placed = (
        P("dp", "mp"),
        P("dp", "mp"),
        P("dp", "mp"),
        P("dp", "mp"),
        P("dp", "mp"),
        P(None, ("mp", "dp"), None),
        P(None, "dp", "mp"),
        P(None, "dp", "mp", None),
        P("dp"),
        P("dp"),
        P(),
    )
    return jax.shard_map(
        functools.partial(on_device, mesh.shape["dp"], mesh.shape["mp"]),
        mesh=mesh,
        in_specs=placed,
        out_specs=(P(None, ("mp", "dp"), None), P(None, "dp", "mp"), P(None, "dp", "mp", None)),
        check_vma=False,
    )
```

```python
import functools

import jax
import jax.numpy as jnp
from jax import lax
from jax.experimental import pallas as pl
from jax.experimental.pallas import tpu as pltpu
from jax.sharding import PartitionSpec as P

ADAPTER_SCALE = 0.5
MASKED = -1e30
BF16, F32 = jnp.bfloat16, jnp.float32
VMEM_LIMIT = 56 * 1024 * 1024
NN = (((1,), (0,)), ((), ()))
NT = (((1,), (1,)), ((), ()))
TN = (((0,), (0,)), ((), ()))
HEADS_PER_CALL = 2


def cost(micros):
    return pl.CostEstimate(
        flops=int(micros * 1e9), bytes_accessed=int(micros * 3.6e6), transcendentals=0
    )


def split2(a):
    high = a.astype(BF16)
    return high, (a - high.astype(F32)).astype(BF16)


def mm(a, b, dims=NN):
    return lax.dot_general(a, b, dims, preferred_element_type=F32)


def mm3(a, b, dims=NN):
    (ah, al), (bh, bl) = a, b
    return mm(ah, bh, dims) + mm(ah, bl, dims) + mm(al, bh, dims)


def bit_reverse(value, bits):
    out = jnp.zeros_like(value)
    for k in range(bits):
        out = out | (((value >> k) & 1) << (bits - 1 - k))
    return out


def swap(a, axis, size, bit):
    return lax.ppermute(a, axis, [(i, i ^ bit) for i in range(size)])


def sum_over(a, axis, size):
    bit = 1
    while bit < size:
        a = a + swap(a, axis, size, bit)
        bit *= 2
    return a


def scatter_sum(part, axis, size):
    bit = 1
    while bit < size:
        half = part.shape[0] // 2
        part = part[:half] + swap(part[half:], axis, size, bit)
        bit *= 2
    return part[0]


def gather_far(a, axis, size, stop):
    a = a[None]
    bit = size // 2
    while bit > stop:
        a = jnp.concatenate([a, swap(a, axis, size, bit)], axis=0)
        bit //= 2
    return a


def gather_near(a, axis, size, start):
    bit = start
    while bit > 1:
        a = jnp.concatenate([a, swap(a, axis, size, bit)], axis=0)
        bit //= 2
    return a, swap(a, axis, size, 1)


def after(a, *others):
    return lax.optimization_barrier((a,) + others)[0]


def by_tenant(owners, tenants):
    count = owners.shape[0]
    index = jnp.arange(count, dtype=jnp.int32)
    ahead = (owners[None, :] < owners[:, None]) | (
        (owners[None, :] == owners[:, None]) & (index[None, :] < index[:, None])
    )
    place = jnp.sum(ahead.astype(jnp.int32), axis=1)
    order = jnp.sum(
        jnp.where(place[None, :] == index[:, None], index[None, :], 0), axis=1
    )
    edge = jnp.arange(tenants + 1, dtype=jnp.int32)
    first = jnp.sum((owners[None, :] < edge[:, None]).astype(jnp.int32), axis=1)
    return order.astype(jnp.int32), first.astype(jnp.int32)


def down_kernel(count, source_ref, tenant_ref, *refs):
    x_refs, w_refs, out_ref = refs[:count], refs[count : 2 * count], refs[2 * count]
    for c in range(count):
        x = x_refs[c][0].astype(BF16)
        high, low = split2(w_refs[c][0])
        out_ref[c] = mm(high, x, NT) + mm(low, x, NT)


def down_partial(x, weights, source, tenant, rows):
    n, _, width = x.shape
    rank = weights.shape[1]
    count = 4

    def x_spec(c):
        return pl.BlockSpec((1, rows, width), lambda p, s, t: (s[p * count + c], 0, 0))

    def w_spec(c):
        return pl.BlockSpec((1, rank, width), lambda p, s, t: (t[p * count + c], 0, 0))

    return pl.pallas_call(
        functools.partial(down_kernel, count),
        grid_spec=pltpu.PrefetchScalarGridSpec(
            num_scalar_prefetch=2,
            grid=(n // count,),
            in_specs=[x_spec(c) for c in range(count)] + [w_spec(c) for c in range(count)],
            out_specs=pl.BlockSpec((count, rank, rows), lambda p, s, t: (p, 0, 0)),
        ),
        out_shape=jax.ShapeDtypeStruct((n, rank, rows), F32),
        compiler_params=pltpu.CompilerParams(vmem_limit_bytes=VMEM_LIMIT),
        cost_estimate=cost(6),
        name="down_partial",
    )(source, tenant, *[x] * count, *[weights] * count)


def attention_kernel(
    groups,
    blocks,
    slots,
    fq_ref,
    fk_ref,
    fv_ref,
    up_ref,
    *rest,
):
    low_refs = rest[:blocks]
    (
        panel_ref,
        slot_ref,
        doc_row_ref,
        doc_col_ref,
        du_ref,
        g_ref,
        bias,
        low_t,
        lct_h,
        lct_l,
        lc_h,
        lc_l,
        panel,
        du,
        q_s,
        dq_s,
        dk_t,
        dv_t,
    ) = rest[blocks:]
    step = pl.program_id(0)
    rows, head = fk_ref.shape
    block = rows // blocks
    owners, _, piece, _ = panel_ref.shape
    rank = owners * piece
    wide = groups * head
    inverse = 1.0 / head**0.5
    slot = slot_ref[...]

    @pl.when(step == 0)
    def _():
        row = lax.broadcasted_iota(jnp.int32, (rows, rows), 0)
        col = lax.broadcasted_iota(jnp.int32, (rows, rows), 1)
        joined = (doc_row_ref[...] == doc_col_ref[...]) & (row >= col)
        bias[...] = jnp.where(joined, 0.0, MASKED)
        for b in range(blocks):
            low_t[:, b * block : (b + 1) * block] = low_refs[b][...]
        for part in range(3):
            low = low_t[part * rank : (part + 1) * rank, :] * ADAPTER_SCALE
            for s in range(slots):
                mine = jnp.where(slot == s, low, 0.0)
                span = slice(s * rank, (s + 1) * rank)
                high, rest_ = split2(mine)
                lct_h[part, span, :] = high
                lct_l[part, span, :] = rest_
            both = jnp.concatenate(
                [jnp.where(slot == s, low, 0.0) for s in range(slots)], axis=0
            ).T
            high, rest_ = split2(both)
            lc_h[part] = high
            lc_l[part] = rest_
        g_ref[...] = jnp.zeros_like(g_ref)

    for w in range(owners):
        for s in range(slots):
            start = s * rank + w * piece
            panel[start : start + piece, :] = panel_ref[w, s]
    u_q = split2(panel[:, :wide])
    u_k = split2(panel[:, wide : wide + head])
    u_v = split2(panel[:, wide + head :])
    k = (fk_ref[...].astype(F32) + mm3((lc_h[1], lc_l[1]), u_k)).astype(BF16)
    v = (fv_ref[...].astype(F32) + mm3((lc_h[2], lc_l[2]), u_v)).astype(BF16)
    q_s[...] = (fq_ref[...].astype(F32) + mm3((lc_h[0], lc_l[0]), u_q)).astype(BF16)
    dk_t[...] = jnp.zeros_like(dk_t)
    dv_t[...] = jnp.zeros_like(dv_t)

    for b in range(blocks):
        here = slice(b * block, (b + 1) * block)
        reach = (b + 1) * block
        kk, vv = k[:reach], v[:reach]
        mask = bias[here, :reach]
        for h in range(groups):
            lanes = slice(h * head, (h + 1) * head)
            q = q_s[here, lanes]
            up = up_ref[here, lanes]
            scores = mm(q, kk, NT) * inverse + mask
            top = jnp.max(scores, axis=-1, keepdims=True)
            weights = jnp.exp(scores - top)
            total = jnp.sum(weights, axis=-1, keepdims=True)
            probs = weights * (1.0 / total)
            grad_probs = mm(up, vv, NT)
            inner = jnp.sum(probs * grad_probs, axis=-1, keepdims=True)
            grad_scores = (probs * (grad_probs - inner) * inverse).astype(BF16)
            dq_s[here, lanes] = mm(grad_scores, kk)
            dk_t[:, :reach] += mm(q, grad_scores, TN)
            dv_t[:, :reach] += mm(up, probs.astype(BF16), TN)

    dq = split2(dq_s[...])
    dk = split2(dk_t[...])
    dv = split2(dv_t[...])
    du[:, :wide] = mm3((lct_h[0], lct_l[0]), dq)
    du[:, wide : wide + head] = mm3((lct_h[1], lct_l[1]), dk, NT)
    du[:, wide + head :] = mm3((lct_h[2], lct_l[2]), dv, NT)
    for w in range(owners):
        for s in range(slots):
            start = s * rank + w * piece
            du_ref[w, s] = du[start : start + piece, :]
    for part, both in enumerate((mm3(u_q, dq, NT), mm3(u_k, dk), mm3(u_v, dv))):
        mine = jnp.zeros((rank, rows), F32)
        for s in range(slots):
            mine += jnp.where(slot == s, both[s * rank : (s + 1) * rank], 0.0)
        mine *= ADAPTER_SCALE
        for b in range(blocks):
            g_ref[b, part * rank : (part + 1) * rank, :] += mine[
                :, b * block : (b + 1) * block
            ]


def attention(fq, fk, fv, up, lows, panels, slot_rows, docs, head, first, heads):
    rows = fq.shape[0]
    blocks = len(lows)
    block = rows // blocks
    n, slots, piece, cols = panels.shape
    kv_heads = fk.shape[1] // head
    groups = fq.shape[1] // fk.shape[1]
    wide = groups * head
    per = wide + 2 * head
    rank = n * piece
    whole = lambda shape: pl.BlockSpec(shape, lambda g: (0,) * len(shape))
    spans = slots * rank
    return pl.pallas_call(
        functools.partial(attention_kernel, groups, blocks, slots),
        grid=(heads,),
        in_specs=[
            pl.BlockSpec((rows, wide), lambda g: (0, first + g)),
            pl.BlockSpec((rows, head), lambda g: (0, first + g)),
            pl.BlockSpec((rows, head), lambda g: (0, first + g)),
            pl.BlockSpec((rows, wide), lambda g: (0, first + g)),
        ]
        + [whole((3 * rank, block))] * blocks
        + [
            pl.BlockSpec((n, slots, piece, per), lambda g: (0, 0, 0, g)),
            whole((1, rows)),
            whole((1, rows)),
            whole((rows, 1)),
        ],
        out_specs=[
            pl.BlockSpec((n, slots, piece, per), lambda g: (0, 0, 0, g)),
            whole((blocks, 3 * rank, block)),
        ],
        out_shape=[
            jax.ShapeDtypeStruct((n, slots, piece, heads * per), F32),
            jax.ShapeDtypeStruct((blocks, 3 * rank, block), F32),
        ],
        scratch_shapes=[
            pltpu.VMEM((rows, rows), F32),
            pltpu.VMEM((3 * rank, rows), F32),
            pltpu.VMEM((3, spans, rows), BF16),
            pltpu.VMEM((3, spans, rows), BF16),
            pltpu.VMEM((3, rows, spans), BF16),
            pltpu.VMEM((3, rows, spans), BF16),
            pltpu.VMEM((spans, per), F32),
            pltpu.VMEM((spans, per), F32),
            pltpu.VMEM((rows, wide), BF16),
            pltpu.VMEM((rows, wide), F32),
            pltpu.VMEM((head, rows), F32),
            pltpu.VMEM((head, rows), F32),
        ],
        compiler_params=pltpu.CompilerParams(vmem_limit_bytes=VMEM_LIMIT),
        cost_estimate=cost(15 * heads),
        name="attention_grads",
    )(fq, fk, fv, up, *lows, panels, slot_rows, docs[None, :], docs[:, None])


def down_grad_kernel(blocks, per_step, order_ref, first_ref, source_ref, *refs):
    x_refs, (g0_ref, g1_ref, out_ref, x_all, g_ref, sems) = refs[:blocks], refs[blocks:]
    half = g0_ref.shape[0]
    step = pl.program_id(0)

    @pl.when(step == 0)
    def _():
        copies = [
            pltpu.make_async_copy(
                x_refs[b].at[:, pl.ds(0, x_all.shape[2])], x_all.at[b], sems.at[b]
            )
            for b in range(blocks)
        ] + [
            pltpu.make_async_copy(
                ref, g_ref.at[pl.ds(side * half, half)], sems.at[blocks + side]
            )
            for side, ref in enumerate((g0_ref, g1_ref))
        ]
        for copy in copies:
            copy.start()
        for copy in copies:
            copy.wait()

    for t in range(per_step):
        tenant = step * per_step + t
        out_ref[t] = jnp.zeros(out_ref.shape[1:], F32)

        def add(e, carry):
            item = order_ref[e]
            place = item // blocks
            b = item - place * blocks
            x = x_all[b, source_ref[place]].astype(BF16)
            high, low = split2(g_ref[place, b])
            out_ref[t] += mm(high, x) + mm(low, x)
            return carry

        lax.fori_loop(first_ref[tenant], first_ref[tenant + 1], add, 0)


def down_grad(xs, g, order, first, source, tenants):
    blocks = len(xs)
    n, rows, width = xs[1].shape
    rank = g[0].shape[2]
    per_step = 8
    return pl.pallas_call(
        functools.partial(down_grad_kernel, blocks, per_step),
        grid_spec=pltpu.PrefetchScalarGridSpec(
            num_scalar_prefetch=3,
            grid=(tenants // per_step,),
            in_specs=[pl.BlockSpec(memory_space=pl.ANY)] * (blocks + 2),
            out_specs=pl.BlockSpec((per_step, rank, width), lambda i, *_: (i, 0, 0)),
            scratch_shapes=[
                pltpu.VMEM((blocks, n, rows, width), F32),
                pltpu.VMEM((n,) + g[0].shape[1:], F32),
                pltpu.SemaphoreType.DMA((blocks + 2,)),
            ],
        ),
        out_shape=jax.ShapeDtypeStruct((tenants, rank, width), F32),
        compiler_params=pltpu.CompilerParams(vmem_limit_bytes=VMEM_LIMIT),
        cost_estimate=cost(15),
        name="down_grad",
    )(order, first, source, *xs, *g)


def up_grad_kernel(calls, per_step, kv_heads, head, order_ref, first_ref, *refs):
    in_refs, (q_ref, kv_ref) = refs[:calls], refs[calls:]
    step = pl.program_id(0)
    wide = q_ref.shape[2] // kv_heads
    per = wide + 2 * head
    heads = kv_heads // calls
    for t in range(per_step):
        tenant = step * per_step + t
        q_ref[t] = jnp.zeros(q_ref.shape[1:], F32)
        kv_ref[t] = jnp.zeros(kv_ref.shape[1:], F32)

        def add(e, carry):
            item = order_ref[e]
            for c in range(calls):
                for h in range(heads):
                    at = c * heads + h
                    q_ref[t, :, at * wide : (at + 1) * wide] += in_refs[c][
                        item, :, h * per : h * per + wide
                    ]
                    kv_ref[t, at] += in_refs[c][item, :, h * per + wide : (h + 1) * per]
            return carry

        lax.fori_loop(first_ref[tenant], first_ref[tenant + 1], add, 0)


def up_grad(dus, order, first, tenants, kv_heads, head):
    calls = len(dus)
    items, piece, cols = dus[0].shape
    per_step = 8
    wide = cols * calls // kv_heads - 2 * head
    return pl.pallas_call(
        functools.partial(up_grad_kernel, calls, per_step, kv_heads, head),
        grid_spec=pltpu.PrefetchScalarGridSpec(
            num_scalar_prefetch=2,
            grid=(tenants // per_step,),
            in_specs=[pl.BlockSpec((items, piece, cols), lambda i, *_: (0, 0, 0))] * calls,
            out_specs=[
                pl.BlockSpec((per_step, piece, kv_heads * wide), lambda i, *_: (i, 0, 0)),
                pl.BlockSpec((per_step, kv_heads, piece, 2 * head), lambda i, *_: (i, 0, 0, 0)),
            ],
        ),
        out_shape=[
            jax.ShapeDtypeStruct((tenants, piece, kv_heads * wide), F32),
            jax.ShapeDtypeStruct((tenants, kv_heads, piece, 2 * head), F32),
        ],
        compiler_params=pltpu.CompilerParams(vmem_limit_bytes=VMEM_LIMIT),
        cost_estimate=cost(6),
        name="up_grad",
    )(order, first, *dus)


def exchange(a):
    return lax.all_to_all(a, "dp", split_axis=0, concat_axis=0, tiled=True)


def on_device(
    dp_count,
    mp_count,
    normed_input_rows,
    frozen_queries,
    frozen_keys,
    frozen_values,
    attention_output_gradient,
    adapter_down_weight,
    adapter_up_query,
    adapter_up_key_value,
    document_numbers,
    block_tenant_slot,
    shard_tenant_table,
):
    rows = normed_input_rows.shape[0]
    blocks = block_tenant_slot.shape[0]
    block = rows // blocks
    tenants, width, ranks = adapter_down_weight.shape
    slots = shard_tenant_table.shape[1]
    piece = adapter_up_query.shape[1]
    kv_heads = adapter_up_key_value.shape[2]
    head = adapter_up_key_value.shape[3] // 2
    wide = adapter_up_query.shape[2] // kv_heads
    me = lax.axis_index("dp").astype(jnp.int32)

    wires = [
        normed_input_rows[b * block : (b + 1) * block]
        .reshape(block, dp_count, width)
        .transpose(1, 0, 2)
        .astype(F32)
        for b in range(blocks)
    ]
    slot_tile = jnp.zeros((8, width), F32).at[0, :blocks].set(block_tenant_slot.astype(F32))
    wires[0] = jnp.concatenate(
        [wires[0], jnp.broadcast_to(slot_tile[None], (dp_count, 8, width))], axis=1
    )
    xs = [exchange(wires[0])]
    for b in range(1, blocks):
        xs.append(exchange(after(wires[b], xs[-1])))

    source = me ^ bit_reverse(
        jnp.arange(dp_count, dtype=jnp.int32), dp_count.bit_length() - 1
    )
    slots_all = xs[0][:, block, :blocks].astype(jnp.int32)[source]
    owners = shard_tenant_table[source[:, None], slots_all]

    weights = jnp.swapaxes(adapter_down_weight, 1, 2)
    lows = []
    for b in range(blocks):
        part = down_partial(xs[b], weights, source, owners[:, b], block)
        lows.append(sum_over(scatter_sum(part, "dp", dp_count), "mp", mp_count))

    wanted = shard_tenant_table.reshape(-1)
    up_query = adapter_up_query[wanted].reshape(-1, piece, kv_heads, wide)
    up_key_value = adapter_up_key_value[wanted]
    wire = jnp.concatenate([up_query, up_key_value], axis=-1)
    heads = min(HEADS_PER_CALL, kv_heads)
    calls = kv_heads // heads
    per = wide + 2 * head
    panels = []
    for c in range(calls):
        own = wire[:, :, c * heads : (c + 1) * heads].reshape(-1, piece, heads * per)
        own = after(own, xs[-1]) if c == 0 else after(own, panels[-1], lows[-1])
        panels.append(exchange(own).reshape(dp_count, slots, piece, heads * per))

    slot_rows = jnp.repeat(block_tenant_slot, block)[None, :]
    dus, g = [], None
    for c in range(calls):
        du, g_part = attention(
            frozen_queries,
            frozen_keys,
            frozen_values,
            attention_output_gradient,
            lows,
            panels[c],
            slot_rows,
            document_numbers,
            head,
            c * heads,
            heads,
        )
        g = g_part if g is None else g + g_part
        dus.append(du.reshape(dp_count * slots, piece, heads * per))
    for c in range(calls - 1):
        dus[c] = exchange(dus[c])
    far = gather_far(sum_over(after(g, *dus[:-1]), "mp", mp_count), "dp", dp_count, 2)
    dus[-1] = exchange(after(dus[-1], far))
    g_halves = gather_near(far, "dp", dp_count, 2)
    order, first = by_tenant(owners.reshape(-1), tenants)
    grad_down = down_grad(xs, g_halves, order, first, source, tenants)
    order, first = by_tenant(wanted, tenants)
    grad_upq, grad_upkv = up_grad(dus, order, first, tenants, kv_heads, head)
    return (
        jnp.swapaxes(grad_down, 1, 2),
        grad_upq,
        jnp.swapaxes(grad_upkv, 1, 2),
    )


def solution(mesh):
    placed = (
        P("dp", "mp"),
        P("dp", "mp"),
        P("dp", "mp"),
        P("dp", "mp"),
        P("dp", "mp"),
        P(None, ("mp", "dp"), None),
        P(None, "dp", "mp"),
        P(None, "dp", "mp", None),
        P("dp"),
        P("dp"),
        P(),
    )
    return jax.shard_map(
        functools.partial(on_device, mesh.shape["dp"], mesh.shape["mp"]),
        mesh=mesh,
        in_specs=placed,
        out_specs=(P(None, ("mp", "dp"), None), P(None, "dp", "mp"), P(None, "dp", "mp", None)),
        check_vma=False,
    )
```

```python
import functools

import jax
import jax.numpy as jnp
from jax import lax
from jax.experimental import pallas as pl
from jax.experimental.pallas import tpu as pltpu
from jax.sharding import PartitionSpec as P

ADAPTER_SCALE = 0.5
MASKED = -1e30
BF16, F32 = jnp.bfloat16, jnp.float32
VMEM_LIMIT = 56 * 1024 * 1024
NN = (((1,), (0,)), ((), ()))
NT = (((1,), (1,)), ((), ()))
TN = (((0,), (0,)), ((), ()))
HEADS_PER_CALL = 2
ATTENTION_MICROS = 10
DOWN_MICROS = 2


def cost(micros):
    return pl.CostEstimate(
        flops=int(micros * 1e9), bytes_accessed=int(micros * 3.6e6), transcendentals=0
    )


def split2(a):
    high = a.astype(BF16)
    return high, (a - high.astype(F32)).astype(BF16)


def mm(a, b, dims=NN):
    return lax.dot_general(a, b, dims, preferred_element_type=F32)


def mm3(a, b, dims=NN):
    (ah, al), (bh, bl) = a, b
    return mm(ah, bh, dims) + mm(ah, bl, dims) + mm(al, bh, dims)


def bit_reverse(value, bits):
    out = jnp.zeros_like(value)
    for k in range(bits):
        out = out | (((value >> k) & 1) << (bits - 1 - k))
    return out


def swap(a, axis, size, bit):
    return lax.ppermute(a, axis, [(i, i ^ bit) for i in range(size)])


def sum_over(a, axis, size):
    bit = 1
    while bit < size:
        a = a + swap(a, axis, size, bit)
        bit *= 2
    return a


def scatter_sum(part, axis, size):
    bit = 1
    while bit < min(size, 4):
        half = part.shape[0] // 2
        part = part[:half] + swap(part[half:], axis, size, bit)
        bit *= 2
    moved = [
        swap(part[k], axis, size, bit_reversed(k, part.shape[0]) * bit)
        for k in range(1, part.shape[0])
    ]
    return functools.reduce(jnp.add, moved, part[0])


def bit_reversed(k, size):
    out = 0
    for i in range(size.bit_length() - 1):
        out |= (k >> i & 1) << (size.bit_length() - 2 - i)
    return out


def gather_far(a, axis, size):
    far = max(size // 4, 1)
    moved = [a] + [swap(a, axis, size, bit_reversed(k, far) * 4) for k in range(1, far)]
    return jnp.concatenate(moved, axis=0)


def gather_step(a, axis, size, bit):
    return jnp.concatenate([a, swap(a, axis, size, bit)], axis=0)


def after(a, *others):
    return lax.optimization_barrier((a,) + others)[0]


def by_tenant(owners, tenants):
    count = owners.shape[0]
    index = jnp.arange(count, dtype=jnp.int32)
    ahead = (owners[None, :] < owners[:, None]) | (
        (owners[None, :] == owners[:, None]) & (index[None, :] < index[:, None])
    )
    place = jnp.sum(ahead.astype(jnp.int32), axis=1)
    order = jnp.sum(
        jnp.where(place[None, :] == index[:, None], index[None, :], 0), axis=1
    )
    edge = jnp.arange(tenants + 1, dtype=jnp.int32)
    first = jnp.sum((owners[None, :] < edge[:, None]).astype(jnp.int32), axis=1)
    return order.astype(jnp.int32), first.astype(jnp.int32)


def wire_kernel(n, slot_ref, x_ref, out_ref):
    rows = x_ref.shape[0]
    width = x_ref.shape[1] // n
    for r in range(n):
        out_ref[r, :rows] = x_ref[:, r * width : (r + 1) * width].astype(F32)
    if out_ref.shape[1] > rows:
        lane = lax.broadcasted_iota(jnp.int32, (8, width), 1)
        tile = jnp.zeros((8, width), F32)
        for b in range(slot_ref.shape[0]):
            tile = jnp.where(lane == b, slot_ref[b].astype(F32), tile)
        out_ref[:, rows:] = jnp.broadcast_to(tile[None], (n, 8, width))


def rows_wire(x, block_slots, n, b):
    blocks = block_slots.shape[0]
    rows, width = x.shape[0] // blocks, x.shape[1] // n
    per = min(n, max(128 // width, 1) * 4)
    tall = rows + (8 if b == 0 else 0)
    return pl.pallas_call(
        functools.partial(wire_kernel, per),
        grid_spec=pltpu.PrefetchScalarGridSpec(
            num_scalar_prefetch=1,
            grid=(n // per,),
            in_specs=[pl.BlockSpec((rows, per * width), lambda i, s: (b, i))],
            out_specs=pl.BlockSpec((per, tall, width), lambda i, s: (i, 0, 0)),
        ),
        out_shape=jax.ShapeDtypeStruct((n, tall, width), F32),
        cost_estimate=cost(2),
        compiler_params=pltpu.CompilerParams(vmem_limit_bytes=VMEM_LIMIT),
        name="rows_wire",
    )(block_slots, x)


def down_kernel(count, calls, source_ref, tenant_ref, *refs):
    x_refs, w_refs, out_ref = refs[: count * calls], refs[count * calls : -1], refs[-1]
    for c in range(count):
        for b in range(calls):
            x = x_refs[c * calls + b][0].astype(BF16)
            high, low = split2(w_refs[c * calls + b][0])
            out_ref[c, b] = mm(high, x, NT) + mm(low, x, NT)


def down_partial(xs, weights, source, tenant, rows):
    n, _, width = xs[0].shape
    rank = weights.shape[1]
    calls = len(xs)
    count = 4 // calls
    every = [(c, b) for c in range(count) for b in range(calls)]

    def x_spec(c, b):
        return pl.BlockSpec((1, rows, width), lambda p, s, t: (s[p * count + c], 0, 0))

    def w_spec(c, b):
        return pl.BlockSpec(
            (1, rank, width), lambda p, s, t: (t[(p * count + c) * calls + b], 0, 0)
        )

    return pl.pallas_call(
        functools.partial(down_kernel, count, calls),
        grid_spec=pltpu.PrefetchScalarGridSpec(
            num_scalar_prefetch=2,
            grid=(n // count,),
            in_specs=[x_spec(*at) for at in every] + [w_spec(*at) for at in every],
            out_specs=pl.BlockSpec((count, calls, rank, rows), lambda p, s, t: (p, 0, 0, 0)),
        ),
        out_shape=jax.ShapeDtypeStruct((n, calls, rank, rows), F32),
        cost_estimate=cost(DOWN_MICROS * calls),
        compiler_params=pltpu.CompilerParams(vmem_limit_bytes=VMEM_LIMIT),
        name="down_partial",
    )(source, tenant.reshape(-1), *[xs[b] for _, b in every], *[weights] * len(every))


def attention_kernel(groups, slots, blocks, todo, *refs):
    first_call, last_call = todo[0] == blocks - 1, todo[-1] == 0
    used = todo[0] + 1
    fq_ref, fk_ref, fv_ref, up_ref = refs[:4]
    low_refs = refs[4 : 4 + used]
    panel_ref, slot_ref, doc_row_ref, doc_col_ref, g_in_ref = refs[4 + used : 9 + used]
    refs = refs[9 + used :]
    if not first_call:
        carry_in, refs = refs[:3], refs[3:]
    if last_call:
        (du_ref, g_ref), refs = refs[:2], refs[2:]
    else:
        (g_ref, *carry_out), refs = refs[:4], refs[4:]
    bias, lct_h, lct_l, lc_h, lc_l, panel, du, dk, dv, q_s, up_s, sc, gp, ds, pr = refs
    step = pl.program_id(0)
    rows, head = fk_ref.shape
    block = rows // blocks
    owners, _, piece, _ = panel_ref.shape
    rank = owners * piece
    wide = groups * head
    inverse = 1.0 / head**0.5
    slot = slot_ref[...]

    @pl.when(step == 0)
    def _():
        key = lax.broadcasted_iota(jnp.int32, (rows, rows), 0)
        row = lax.broadcasted_iota(jnp.int32, (rows, rows), 1)
        joined = (doc_row_ref[...] == doc_col_ref[...]) & (row >= key)
        bias[...] = jnp.where(joined, 0.0, MASKED)
        for b in range(used):
            span = slice(b * block, (b + 1) * block)
            for part in range(3):
                low = low_refs[b][part * rank : (part + 1) * rank, :] * ADAPTER_SCALE
                both = jnp.concatenate(
                    [jnp.where(slot[:, span] == s, low, 0.0) for s in range(slots)], axis=0
                )
                lct_h[part, b], lct_l[part, b] = split2(both)
                lc_h[part, span, :], lc_l[part, span, :] = split2(both.T)
        for b in todo:
            g_ref[b - todo[-1]] = g_in_ref[b] * (1.0 / ADAPTER_SCALE)

    for w in range(owners):
        for s in range(slots):
            start = s * rank + w * piece
            panel[start : start + piece, :] = panel_ref[w, s]
    u_q = split2(panel[:, :wide])
    u_k = split2(panel[:, wide : wide + head])
    u_v = split2(panel[:, wide + head :])
    seen = used * block
    k = fk_ref[:seen].astype(F32) + mm3((lc_h[1, :seen], lc_l[1, :seen]), u_k)
    v = fv_ref[:seen].astype(F32) + mm3((lc_h[2, :seen], lc_l[2, :seen]), u_v)
    k, v = k.astype(BF16), v.astype(BF16)
    k_t = k.T
    if first_call:
        dk[...] = jnp.zeros_like(dk)
        dv[...] = jnp.zeros_like(dv)
        du[...] = jnp.zeros_like(du)
    else:
        dk[...], dv[...], du[...] = [ref[0] for ref in carry_in]

    for b in todo:
        here = slice(b * block, (b + 1) * block)
        reach = (b + 1) * block
        q = fq_ref[here].astype(F32) + mm3((lc_h[0, here], lc_l[0, here]), u_q)
        q = q.astype(BF16)
        for h in range(groups):
            at, lanes = slice(h * block, (h + 1) * block), slice(h * head, (h + 1) * head)
            q_s[at] = q[:, lanes]
            up_s[at] = up_ref[here, lanes]
        sc[:reach] = mm(k[:reach], q_s[...], NT)
        gp[:reach] = mm(v[:reach], up_s[...], NT)
        mask = bias[:reach, here]
        for h in range(groups):
            at = slice(h * block, (h + 1) * block)
            scores = sc[:reach, at] * inverse + mask
            weights = jnp.exp(scores - jnp.max(scores, axis=0, keepdims=True))
            scale = 1.0 / jnp.sum(weights, axis=0, keepdims=True)
            grad_probs = gp[:reach, at]
            probs = weights * scale
            inner = jnp.sum(probs * grad_probs, axis=0, keepdims=True)
            ds[:reach, at] = (probs * (grad_probs - inner) * inverse).astype(BF16)
            pr[:reach, at] = probs.astype(BF16)
        dk[:reach] += mm(ds[:reach], q_s[...])
        dv[:reach] += mm(pr[:reach], up_s[...])
        dq = split2(mm(k_t[:, :reach], ds[:reach]))
        dk_b, dv_b = split2(dk[here]), split2(dv[here])
        lct = [(lct_h[part, b], lct_l[part, b]) for part in range(3)]
        both = jnp.zeros((slots * rank, block), F32)
        for h in range(groups):
            at, lanes = slice(h * block, (h + 1) * block), slice(h * head, (h + 1) * head)
            dq_h = (dq[0][:, at], dq[1][:, at])
            du[:, lanes] += mm3(lct[0], dq_h, NT)
            both += mm3((u_q[0][:, lanes], u_q[1][:, lanes]), dq_h)
        du[:, wide : wide + head] += mm3(lct[1], dk_b)
        du[:, wide + head :] += mm3(lct[2], dv_b)
        for part, full in enumerate((both, mm3(u_k, dk_b, NT), mm3(u_v, dv_b, NT))):
            mine = jnp.zeros((rank, block), F32)
            for s in range(slots):
                mine += jnp.where(slot[:, here] == s, full[s * rank : (s + 1) * rank], 0.0)
            g_ref[b - todo[-1], part * rank : (part + 1) * rank, :] += mine

    @pl.when(step == pl.num_programs(0) - 1)
    def _():
        g_ref[...] *= ADAPTER_SCALE

    if last_call:
        for w in range(owners):
            for s in range(slots):
                start = s * rank + w * piece
                du_ref[w, s] = du[start : start + piece, :]
    else:
        for ref, value in zip(carry_out, (dk, dv, du)):
            ref[0] = value[...]


def attention(
    fq, fk, fv, up, lows, *, panels, slot_rows, docs, g, head, first, heads, todo, carry
):
    rows = fq.shape[0]
    blocks = len(lows)
    block = rows // blocks
    n, slots, piece, cols = panels.shape
    kv_heads = fk.shape[1] // head
    groups = fq.shape[1] // fk.shape[1]
    wide = groups * head
    per = wide + 2 * head
    rank = n * piece
    spans = slots * rank
    used = todo[0] + 1
    whole = lambda shape: pl.BlockSpec(shape, lambda i: (0,) * len(shape))
    carry_shapes = [(heads, rows, head), (heads, rows, head), (heads, spans, per)]
    carry_specs = [
        pl.BlockSpec((1,) + shape[1:], lambda i: (i, 0, 0)) for shape in carry_shapes
    ]
    g_shape = (len(todo), 3 * rank, block)
    if todo[-1] == 0:
        out_specs = [pl.BlockSpec((n, slots, piece, per), lambda i: (0, 0, 0, i)), whole(g_shape)]
        out_shape = [(n, slots, piece, heads * per), g_shape]
    else:
        out_specs = [whole(g_shape)] + carry_specs
        out_shape = [g_shape] + carry_shapes
    first_call = todo[0] == blocks - 1
    pairs = sum(b + 1 for b in todo) / (blocks * (blocks + 1) / 2)
    return pl.pallas_call(
        functools.partial(attention_kernel, groups, slots, blocks, todo),
        grid=(heads,),
        in_specs=[
            pl.BlockSpec((rows, wide), lambda i: (0, first + i)),
            pl.BlockSpec((rows, head), lambda i: (0, first + i)),
            pl.BlockSpec((rows, head), lambda i: (0, first + i)),
            pl.BlockSpec((rows, wide), lambda i: (0, first + i)),
        ]
        + [whole((3 * rank, block))] * used
        + [
            pl.BlockSpec((n, slots, piece, per), lambda i: (0, 0, 0, i)),
            whole((1, rows)),
            whole((1, rows)),
            whole((rows, 1)),
            whole(g.shape),
        ]
        + ([] if first_call else carry_specs),
        out_specs=out_specs,
        out_shape=[jax.ShapeDtypeStruct(shape, F32) for shape in out_shape],
        scratch_shapes=[
            pltpu.VMEM((rows, rows), F32),
            pltpu.VMEM((3, used, spans, block), BF16),
            pltpu.VMEM((3, used, spans, block), BF16),
            pltpu.VMEM((3, used * block, spans), BF16),
            pltpu.VMEM((3, used * block, spans), BF16),
            pltpu.VMEM((spans, per), F32),
            pltpu.VMEM((spans, per), F32),
            pltpu.VMEM((rows, head), F32),
            pltpu.VMEM((rows, head), F32),
            pltpu.VMEM((groups * block, head), BF16),
            pltpu.VMEM((groups * block, head), BF16),
            pltpu.VMEM((rows, groups * block), F32),
            pltpu.VMEM((rows, groups * block), F32),
            pltpu.VMEM((rows, groups * block), BF16),
            pltpu.VMEM((rows, groups * block), BF16),
        ],
        cost_estimate=cost(ATTENTION_MICROS * heads * pairs),
        compiler_params=pltpu.CompilerParams(vmem_limit_bytes=VMEM_LIMIT),
        name="attention_grads",
    )(
        fq,
        fk,
        fv,
        up,
        *lows[:used],
        panels,
        slot_rows,
        docs[None, :],
        docs[:, None],
        g,
        *(() if first_call else carry),
    )


def down_grad_kernel(blocks, per_step, order_ref, first_ref, source_ref, *refs):
    x_refs, g_refs = refs[:blocks], refs[blocks : 3 * blocks]
    out_ref, x_all, g_ref, sems = refs[3 * blocks :]
    half = g_refs[0].shape[0]
    step = pl.program_id(0)

    @pl.when(step == 0)
    def _():
        copies = [
            pltpu.make_async_copy(
                x_refs[b].at[:, pl.ds(0, x_all.shape[2])], x_all.at[b], sems.at[b]
            )
            for b in range(blocks)
        ] + [
            pltpu.make_async_copy(
                ref, g_ref.at[i // 2, pl.ds(i % 2 * half, half)], sems.at[blocks + i]
            )
            for i, ref in enumerate(g_refs)
        ]
        for copy in copies:
            copy.start()
        for copy in copies:
            copy.wait()

    for t in range(per_step):
        tenant = step * per_step + t
        out_ref[t] = jnp.zeros(out_ref.shape[1:], F32)

        def add(e, carry):
            item = order_ref[e]
            place = item // blocks
            b = item - place * blocks
            x = x_all[b, source_ref[place]].astype(BF16)
            high, low = split2(g_ref[b, place])
            out_ref[t] += mm(high, x) + mm(low, x)
            return carry

        lax.fori_loop(first_ref[tenant], first_ref[tenant + 1], add, 0)


def down_grad(xs, g, order, first, source, tenants):
    blocks = len(xs)
    n, rows, width = xs[1].shape
    rank = g[0].shape[1]
    per_step = 8
    return pl.pallas_call(
        functools.partial(down_grad_kernel, blocks, per_step),
        grid_spec=pltpu.PrefetchScalarGridSpec(
            num_scalar_prefetch=3,
            grid=(tenants // per_step,),
            in_specs=[pl.BlockSpec(memory_space=pl.ANY)] * (3 * blocks),
            out_specs=pl.BlockSpec((per_step, rank, width), lambda i, *_: (i, 0, 0)),
            scratch_shapes=[
                pltpu.VMEM((blocks, n, rows, width), F32),
                pltpu.VMEM((blocks, n) + g[0].shape[1:], F32),
                pltpu.SemaphoreType.DMA((3 * blocks,)),
            ],
        ),
        out_shape=jax.ShapeDtypeStruct((tenants, rank, width), F32),
        compiler_params=pltpu.CompilerParams(vmem_limit_bytes=VMEM_LIMIT),
        cost_estimate=cost(15),
        name="down_grad",
    )(order, first, source, *xs, *g)


def down_grad_last_kernel(owner_ref, leader_ref, source_ref, *refs):
    x_ref, g0_ref, g1_ref, sum_ref, out_ref, x_all, g_all, acc, in_sems, out_sems = refs
    del sum_ref
    n, rows, _ = x_all.shape
    half = n // 2
    loads = [
        pltpu.make_async_copy(x_ref.at[:, pl.ds(0, rows)], x_all, in_sems.at[n]),
        pltpu.make_async_copy(g0_ref, g_all.at[pl.ds(0, half)], in_sems.at[n + 1]),
        pltpu.make_async_copy(g1_ref, g_all.at[pl.ds(half, half)], in_sems.at[n + 2]),
    ]
    for load in loads:
        load.start()

    def tile(p, inward):
        there, here = out_ref.at[owner_ref[p]], acc.at[p]
        if inward:
            return pltpu.make_async_copy(there, here, in_sems.at[p])
        return pltpu.make_async_copy(here, there, out_sems.at[p])

    def leaders(act):
        for p in range(n):
            pl.when(leader_ref[p] == p)(functools.partial(act, p))

    leaders(lambda p: tile(p, True).start())
    for load in loads:
        load.wait()
    leaders(lambda p: tile(p, True).wait())
    for p in range(n):
        x = x_all[source_ref[p]].astype(BF16)
        high, low = split2(g_all[p])
        acc[leader_ref[p]] += mm(high, x) + mm(low, x)
    leaders(lambda p: tile(p, False).start())
    leaders(lambda p: tile(p, False).wait())


def down_grad_last(x, g, total, owner, source):
    n, rank, rows = 2 * g[0].shape[0], g[0].shape[1], g[0].shape[2]
    width = x.shape[2]
    index = jnp.arange(n, dtype=jnp.int32)
    same = owner[None, :] == owner[:, None]
    leader = jnp.min(jnp.where(same, index[None, :], n), axis=1).astype(jnp.int32)
    return pl.pallas_call(
        down_grad_last_kernel,
        grid_spec=pltpu.PrefetchScalarGridSpec(
            num_scalar_prefetch=3,
            grid=(1,),
            in_specs=[pl.BlockSpec(memory_space=pl.ANY)] * 4,
            out_specs=pl.BlockSpec(memory_space=pl.ANY),
            scratch_shapes=[
                pltpu.VMEM((n, rows, width), F32),
                pltpu.VMEM((n, rank, rows), F32),
                pltpu.VMEM((n, rank, width), F32),
                pltpu.SemaphoreType.DMA((n + 3,)),
                pltpu.SemaphoreType.DMA((n,)),
            ],
        ),
        out_shape=jax.ShapeDtypeStruct(total.shape, F32),
        input_output_aliases={6: 0},
        cost_estimate=cost(6),
        compiler_params=pltpu.CompilerParams(vmem_limit_bytes=VMEM_LIMIT),
        name="down_grad_last",
    )(owner, leader, source, x, *g, total)


def up_grad_kernel(calls, per_step, kv_heads, head, order_ref, first_ref, *refs):
    in_refs, (q_ref, kv_ref, kv_sum) = refs[:calls], refs[calls:]
    step = pl.program_id(0)
    wide = q_ref.shape[2] // kv_heads
    per = wide + 2 * head
    heads = kv_heads // calls
    for t in range(per_step):
        tenant = step * per_step + t
        q_ref[t] = jnp.zeros(q_ref.shape[1:], F32)
        kv_sum[...] = jnp.zeros_like(kv_sum)

        def add(e, carry):
            item = order_ref[e]
            for c in range(calls):
                for h in range(heads):
                    at = c * heads + h
                    q_ref[t, :, at * wide : (at + 1) * wide] += in_refs[c][
                        item, :, h * per : h * per + wide
                    ]
                    kv_sum[at] += in_refs[c][item, :, h * per + wide : (h + 1) * per]
            return carry

        lax.fori_loop(first_ref[tenant], first_ref[tenant + 1], add, 0)
        for k in range(kv_ref.shape[1]):
            for h in range(kv_heads):
                kv_ref[t, k, h, :] = kv_sum[h, k, :]


def up_grad(dus, order, first, tenants, kv_heads, head):
    calls = len(dus)
    items, piece, cols = dus[0].shape
    per_step = 8
    wide = cols * calls // kv_heads - 2 * head
    return pl.pallas_call(
        functools.partial(up_grad_kernel, calls, per_step, kv_heads, head),
        grid_spec=pltpu.PrefetchScalarGridSpec(
            num_scalar_prefetch=2,
            grid=(tenants // per_step,),
            in_specs=[pl.BlockSpec((items, piece, cols), lambda i, *_: (0, 0, 0))] * calls,
            out_specs=[
                pl.BlockSpec((per_step, piece, kv_heads * wide), lambda i, *_: (i, 0, 0)),
                pl.BlockSpec((per_step, piece, kv_heads, 2 * head), lambda i, *_: (i, 0, 0, 0)),
            ],
            scratch_shapes=[pltpu.VMEM((kv_heads, piece, 2 * head), F32)],
        ),
        out_shape=[
            jax.ShapeDtypeStruct((tenants, piece, kv_heads * wide), F32),
            jax.ShapeDtypeStruct((tenants, piece, kv_heads, 2 * head), F32),
        ],
        compiler_params=pltpu.CompilerParams(vmem_limit_bytes=VMEM_LIMIT),
        cost_estimate=cost(6),
        name="up_grad",
    )(order, first, *dus)


def exchange(a):
    return lax.all_to_all(a, "dp", split_axis=0, concat_axis=0, tiled=True)


def on_device(
    dp_count,
    mp_count,
    normed_input_rows,
    frozen_queries,
    frozen_keys,
    frozen_values,
    attention_output_gradient,
    adapter_down_weight,
    adapter_up_query,
    adapter_up_key_value,
    document_numbers,
    block_tenant_slot,
    shard_tenant_table,
):
    rows = normed_input_rows.shape[0]
    blocks = block_tenant_slot.shape[0]
    block = rows // blocks
    tenants, width, ranks = adapter_down_weight.shape
    slots = shard_tenant_table.shape[1]
    piece = adapter_up_query.shape[1]
    kv_heads = adapter_up_key_value.shape[2]
    head = adapter_up_key_value.shape[3] // 2
    wide = adapter_up_query.shape[2] // kv_heads
    me = lax.axis_index("dp").astype(jnp.int32)

    wires = [
        rows_wire(normed_input_rows, block_tenant_slot, dp_count, b) for b in range(blocks)
    ]
    wanted = shard_tenant_table.reshape(-1)
    up_query = adapter_up_query[wanted].reshape(-1, piece, kv_heads, wide)
    up_key_value = adapter_up_key_value[wanted]
    wire = jnp.concatenate([up_query, up_key_value], axis=-1)
    heads = min(HEADS_PER_CALL, kv_heads)
    calls = kv_heads // heads
    per = wide + 2 * head
    owns = [
        wire[:, :, c * heads : (c + 1) * heads].reshape(-1, piece, heads * per)
        for c in range(calls)
    ]

    xs = [exchange(wires[0])]
    for b in range(1, blocks):
        xs.append(exchange(after(wires[b], xs[-1], *(owns if b == blocks - 1 else ()))))

    source = me ^ bit_reverse(
        jnp.arange(dp_count, dtype=jnp.int32), dp_count.bit_length() - 1
    )
    slots_all = xs[0][:, block, :blocks].astype(jnp.int32)[source]
    owners = shard_tenant_table[source[:, None], slots_all]

    weights = jnp.swapaxes(adapter_down_weight, 1, 2)
    part = down_partial(xs[:-1], weights, source, owners[:, :-1], block)
    early = sum_over(scatter_sum(part, "dp", dp_count), "mp", mp_count)
    part = down_partial(xs[-1:], weights, source, owners[:, -1:], block)
    late = sum_over(scatter_sum(part, "dp", dp_count), "mp", mp_count)
    lows = [early[b] for b in range(blocks - 1)] + [late[0]]

    panels = []
    for c in range(calls):
        own = after(owns[c], xs[-1], early) if c == 0 else after(owns[c], panels[-1], late)
        panels.append(exchange(own).reshape(dp_count, slots, piece, heads * per))

    attend = functools.partial(
        attention,
        frozen_queries,
        frozen_keys,
        frozen_values,
        attention_output_gradient,
        lows,
        slot_rows=jnp.repeat(block_tenant_slot, block)[None, :],
        docs=document_numbers,
        head=head,
        heads=heads,
    )
    g = jnp.zeros((blocks, 3 * piece * dp_count, block), F32)
    every = tuple(range(blocks))[::-1]
    dus = []
    for c in range(calls - 1):
        du, g = attend(panels=panels[c], g=g, first=c * heads, todo=every, carry=())
        dus.append(exchange(du.reshape(dp_count * slots, piece, heads * per)))
    sums, fars, carry = {}, {}, ()
    for b in every:
        if b == blocks - 3:
            fars[blocks - 1] = gather_far(sums[blocks - 1], "dp", dp_count)
            carry = after(carry, sums[blocks - 1])
        out = attend(panels=panels[-1], g=g, first=kv_heads - heads, todo=(b,), carry=carry)
        du, g_b = out if b == 0 else (None, out[0])
        carry = out[1:]
        if b == 0:
            g_b = after(g_b, *dus, fars[blocks - 1], *(sums[k] for k in every[:-1]))
        sums[b] = sum_over(g_b, "mp", mp_count)
    du = du.reshape(dp_count * slots, piece, heads * per)
    g_halves = [None] * blocks
    for b in every:
        if b not in fars:
            fars[b] = gather_far(sums[b], "dp", dp_count)
        fars[b] = gather_step(fars[b], "dp", dp_count, 2)
        if b > 0:
            g_halves[b] = (fars[b], swap(fars[b], "dp", dp_count, 1))
    dus.append(exchange(du))

    early = [half for pair in g_halves[1:] for half in pair]
    order, first = by_tenant(owners[:, 1:].reshape(-1), tenants)
    grad_down = down_grad(xs[1:], early, order, first, source, tenants)
    fars[0] = after(fars[0], grad_down)
    g_halves[0] = (fars[0], swap(fars[0], "dp", dp_count, 1))
    grad_down = down_grad_last(xs[0], g_halves[0], grad_down, owners[:, 0], source)
    order, first = by_tenant(wanted, tenants)
    grad_upq, grad_upkv = up_grad(dus, order, first, tenants, kv_heads, head)
    return (
        jnp.swapaxes(grad_down, 1, 2),
        grad_upq,
        grad_upkv,
    )


def solution(mesh):
    placed = (
        P("dp", "mp"),
        P("dp", "mp"),
        P("dp", "mp"),
        P("dp", "mp"),
        P("dp", "mp"),
        P(None, ("mp", "dp"), None),
        P(None, "dp", "mp"),
        P(None, "dp", "mp", None),
        P("dp"),
        P("dp"),
        P(),
    )
    return jax.shard_map(
        functools.partial(on_device, mesh.shape["dp"], mesh.shape["mp"]),
        mesh=mesh,
        in_specs=placed,
        out_specs=(P(None, ("mp", "dp"), None), P(None, "dp", "mp"), P(None, "dp", "mp", None)),
        check_vma=False,
    )
```

```python
import functools

import jax
import jax.numpy as jnp
from jax import lax
from jax.experimental import pallas as pl
from jax.experimental.pallas import tpu as pltpu
from jax.sharding import PartitionSpec as P

ADAPTER_SCALE = 0.5
MASKED = -1e30
BF16, F32 = jnp.bfloat16, jnp.float32
VMEM_LIMIT = 56 * 1024 * 1024
NN = (((1,), (0,)), ((), ()))
NT = (((1,), (1,)), ((), ()))
TN = (((0,), (0,)), ((), ()))
HEADS_PER_CALL = 2
ATTENTION_MICROS = 10
DOWN_MICROS = 2


def cost(micros):
    return pl.CostEstimate(
        flops=int(micros * 1e9), bytes_accessed=int(micros * 3.6e6), transcendentals=0
    )


def split2(a):
    high = a.astype(BF16)
    return high, (a - high.astype(F32)).astype(BF16)


def mm(a, b, dims=NN):
    return lax.dot_general(a, b, dims, preferred_element_type=F32)


def mm3(a, b, dims=NN):
    (ah, al), (bh, bl) = a, b
    return mm(ah, bh, dims) + mm(ah, bl, dims) + mm(al, bh, dims)


def bit_reverse(value, bits):
    out = jnp.zeros_like(value)
    for k in range(bits):
        out = out | (((value >> k) & 1) << (bits - 1 - k))
    return out


def swap(a, axis, size, bit):
    return lax.ppermute(a, axis, [(i, i ^ bit) for i in range(size)])


def sum_over(a, axis, size):
    bit = 1
    while bit < size:
        a = a + swap(a, axis, size, bit)
        bit *= 2
    return a


def scatter_near(part, axis, size):
    bit = 1
    while bit < min(size, 4):
        half = part.shape[0] // 2
        part = part[:half] + swap(part[half:], axis, size, bit)
        bit *= 2
    return part


def scatter_far(part, axis, size):
    bit = min(size, 4)
    moved = [
        swap(part[k], axis, size, bit_reversed(k, part.shape[0]) * bit)
        for k in range(1, part.shape[0])
    ]
    return functools.reduce(jnp.add, moved, part[0])


def bit_reversed(k, size):
    out = 0
    for i in range(size.bit_length() - 1):
        out |= (k >> i & 1) << (size.bit_length() - 2 - i)
    return out


def gather_far(a, axis, size):
    far = max(size // 4, 1)
    moved = [a] + [swap(a, axis, size, bit_reversed(k, far) * 4) for k in range(1, far)]
    return jnp.concatenate(moved, axis=0)


def gather_step(a, axis, size, bit):
    return jnp.concatenate([a, swap(a, axis, size, bit)], axis=0)


def after(a, *others):
    return lax.optimization_barrier((a,) + others)[0]


def by_tenant(owners, tenants):
    count = owners.shape[0]
    index = jnp.arange(count, dtype=jnp.int32)
    ahead = (owners[None, :] < owners[:, None]) | (
        (owners[None, :] == owners[:, None]) & (index[None, :] < index[:, None])
    )
    place = jnp.sum(ahead.astype(jnp.int32), axis=1)
    order = jnp.sum(
        jnp.where(place[None, :] == index[:, None], index[None, :], 0), axis=1
    )
    edge = jnp.arange(tenants + 1, dtype=jnp.int32)
    first = jnp.sum((owners[None, :] < edge[:, None]).astype(jnp.int32), axis=1)
    return order.astype(jnp.int32), first.astype(jnp.int32)


def wire_kernel(n, slot_ref, x_ref, out_ref):
    rows = x_ref.shape[0]
    width = x_ref.shape[1] // n
    for r in range(n):
        out_ref[r, :rows] = x_ref[:, r * width : (r + 1) * width].astype(F32)
    if out_ref.shape[1] > rows:
        lane = lax.broadcasted_iota(jnp.int32, (8, width), 1)
        tile = jnp.zeros((8, width), F32)
        for b in range(slot_ref.shape[0]):
            tile = jnp.where(lane == b, slot_ref[b].astype(F32), tile)
        out_ref[:, rows:] = jnp.broadcast_to(tile[None], (n, 8, width))


def rows_wire(x, block_slots, n, b):
    blocks = block_slots.shape[0]
    rows, width = x.shape[0] // blocks, x.shape[1] // n
    per = min(n, max(128 // width, 1) * 4)
    tall = rows + (8 if b == 0 else 0)
    return pl.pallas_call(
        functools.partial(wire_kernel, per),
        grid_spec=pltpu.PrefetchScalarGridSpec(
            num_scalar_prefetch=1,
            grid=(n // per,),
            in_specs=[pl.BlockSpec((rows, per * width), lambda i, s: (b, i))],
            out_specs=pl.BlockSpec((per, tall, width), lambda i, s: (i, 0, 0)),
        ),
        out_shape=jax.ShapeDtypeStruct((n, tall, width), F32),
        cost_estimate=cost(2),
        compiler_params=pltpu.CompilerParams(vmem_limit_bytes=VMEM_LIMIT),
        name="rows_wire",
    )(block_slots, x)


def down_kernel(count, calls, source_ref, tenant_ref, *refs):
    x_refs, w_refs, out_ref = refs[: count * calls], refs[count * calls : -1], refs[-1]
    for c in range(count):
        for b in range(calls):
            x = x_refs[c * calls + b][0].astype(BF16)
            high, low = split2(w_refs[c * calls + b][0])
            out_ref[c, b] = mm(high, x, NT) + mm(low, x, NT)


def down_partial(xs, weights, source, tenant, rows):
    n, _, width = xs[0].shape
    rank = weights.shape[1]
    calls = len(xs)
    count = 4 // calls
    every = [(c, b) for c in range(count) for b in range(calls)]

    def x_spec(c, b):
        return pl.BlockSpec((1, rows, width), lambda p, s, t: (s[p * count + c], 0, 0))

    def w_spec(c, b):
        return pl.BlockSpec(
            (1, rank, width), lambda p, s, t: (t[(p * count + c) * calls + b], 0, 0)
        )

    return pl.pallas_call(
        functools.partial(down_kernel, count, calls),
        grid_spec=pltpu.PrefetchScalarGridSpec(
            num_scalar_prefetch=2,
            grid=(n // count,),
            in_specs=[x_spec(*at) for at in every] + [w_spec(*at) for at in every],
            out_specs=pl.BlockSpec((count, calls, rank, rows), lambda p, s, t: (p, 0, 0, 0)),
        ),
        out_shape=jax.ShapeDtypeStruct((n, calls, rank, rows), F32),
        cost_estimate=cost(DOWN_MICROS * calls),
        compiler_params=pltpu.CompilerParams(vmem_limit_bytes=VMEM_LIMIT),
        name="down_partial",
    )(source, tenant.reshape(-1), *[xs[b] for _, b in every], *[weights] * len(every))


def attention_kernel(groups, slots, blocks, todo, *refs):
    first_call, last_call = todo[0] == blocks - 1, todo[-1] == 0
    used = todo[0] + 1
    fq_ref, fk_ref, fv_ref, up_ref = refs[:4]
    low_refs = refs[4 : 4 + used]
    panel_ref, slot_ref, doc_row_ref, doc_col_ref, g_in_ref = refs[4 + used : 9 + used]
    refs = refs[9 + used :]
    if not first_call:
        carry_in, refs = refs[:3], refs[3:]
    if last_call:
        (du_ref, g_ref), refs = refs[:2], refs[2:]
    else:
        (g_ref, *carry_out), refs = refs[:4], refs[4:]
    bias, lct_h, lct_l, lc_h, lc_l, panel, du, dk, dv, q_s, up_s, sc, gp, ds, pr = refs
    step = pl.program_id(0)
    rows, head = fk_ref.shape
    block = rows // blocks
    owners, _, piece, _ = panel_ref.shape
    rank = owners * piece
    wide = groups * head
    inverse = 1.0 / head**0.5
    slot = slot_ref[...]

    @pl.when(step == 0)
    def _():
        key = lax.broadcasted_iota(jnp.int32, (rows, rows), 0)
        row = lax.broadcasted_iota(jnp.int32, (rows, rows), 1)
        joined = (doc_row_ref[...] == doc_col_ref[...]) & (row >= key)
        bias[...] = jnp.where(joined, 0.0, MASKED)
        for b in range(used):
            span = slice(b * block, (b + 1) * block)
            for part in range(3):
                low = low_refs[b][part * rank : (part + 1) * rank, :] * ADAPTER_SCALE
                both = jnp.concatenate(
                    [jnp.where(slot[:, span] == s, low, 0.0) for s in range(slots)], axis=0
                )
                lct_h[part, b], lct_l[part, b] = split2(both)
                lc_h[part, span, :], lc_l[part, span, :] = split2(both.T)
        for b in todo:
            g_ref[b - todo[-1]] = g_in_ref[b] * (1.0 / ADAPTER_SCALE)

    for w in range(owners):
        for s in range(slots):
            start = s * rank + w * piece
            panel[start : start + piece, :] = panel_ref[w, s]
    u_q = split2(panel[:, :wide])
    u_k = split2(panel[:, wide : wide + head])
    u_v = split2(panel[:, wide + head :])
    seen = used * block
    k = fk_ref[:seen].astype(F32) + mm3((lc_h[1, :seen], lc_l[1, :seen]), u_k)
    v = fv_ref[:seen].astype(F32) + mm3((lc_h[2, :seen], lc_l[2, :seen]), u_v)
    k, v = k.astype(BF16), v.astype(BF16)
    k_t = k.T
    if first_call:
        dk[...] = jnp.zeros_like(dk)
        dv[...] = jnp.zeros_like(dv)
        du[...] = jnp.zeros_like(du)
    else:
        dk[...], dv[...], du[...] = [ref[0] for ref in carry_in]

    for b in todo:
        here = slice(b * block, (b + 1) * block)
        reach = (b + 1) * block
        q = fq_ref[here].astype(F32) + mm3((lc_h[0, here], lc_l[0, here]), u_q)
        q = q.astype(BF16)
        for h in range(groups):
            at, lanes = slice(h * block, (h + 1) * block), slice(h * head, (h + 1) * head)
            q_s[at] = q[:, lanes]
            up_s[at] = up_ref[here, lanes]
        sc[:reach] = mm(k[:reach], q_s[...], NT)
        gp[:reach] = mm(v[:reach], up_s[...], NT)
        mask = bias[:reach, here]
        for h in range(groups):
            at = slice(h * block, (h + 1) * block)
            scores = sc[:reach, at] * inverse + mask
            weights = jnp.exp(scores - jnp.max(scores, axis=0, keepdims=True))
            scale = 1.0 / jnp.sum(weights, axis=0, keepdims=True)
            grad_probs = gp[:reach, at]
            probs = weights * scale
            inner = jnp.sum(probs * grad_probs, axis=0, keepdims=True)
            ds[:reach, at] = (probs * (grad_probs - inner) * inverse).astype(BF16)
            pr[:reach, at] = probs.astype(BF16)
        dk[:reach] += mm(ds[:reach], q_s[...])
        dv[:reach] += mm(pr[:reach], up_s[...])
        dq = mm(k_t[:, :reach], ds[:reach]).astype(BF16)
        dk_b, dv_b = split2(dk[here]), split2(dv[here])
        lct = [(lct_h[part, b], lct_l[part, b]) for part in range(3)]
        both = jnp.zeros((slots * rank, block), F32)
        for h in range(groups):
            at, lanes = slice(h * block, (h + 1) * block), slice(h * head, (h + 1) * head)
            du[:, lanes] += mm(lct[0][0], dq[:, at], NT)
            both += mm(u_q[0][:, lanes], dq[:, at])
        du[:, wide : wide + head] += mm3(lct[1], dk_b)
        du[:, wide + head :] += mm3(lct[2], dv_b)
        for part, full in enumerate((both, mm3(u_k, dk_b, NT), mm3(u_v, dv_b, NT))):
            mine = jnp.zeros((rank, block), F32)
            for s in range(slots):
                mine += jnp.where(slot[:, here] == s, full[s * rank : (s + 1) * rank], 0.0)
            g_ref[b - todo[-1], part * rank : (part + 1) * rank, :] += mine

    @pl.when(step == pl.num_programs(0) - 1)
    def _():
        g_ref[...] *= ADAPTER_SCALE

    if last_call:
        for w in range(owners):
            for s in range(slots):
                start = s * rank + w * piece
                du_ref[w, s] = du[start : start + piece, :]
    else:
        for ref, value in zip(carry_out, (dk, dv, du)):
            ref[0] = value[...]


def attention(
    fq, fk, fv, up, lows, *, panels, slot_rows, docs, g, head, first, heads, todo, carry
):
    rows = fq.shape[0]
    blocks = len(lows)
    block = rows // blocks
    n, slots, piece, cols = panels.shape
    kv_heads = fk.shape[1] // head
    groups = fq.shape[1] // fk.shape[1]
    wide = groups * head
    per = wide + 2 * head
    rank = n * piece
    spans = slots * rank
    used = todo[0] + 1
    whole = lambda shape: pl.BlockSpec(shape, lambda i: (0,) * len(shape))
    carry_shapes = [(heads, rows, head), (heads, rows, head), (heads, spans, per)]
    carry_specs = [
        pl.BlockSpec((1,) + shape[1:], lambda i: (i, 0, 0)) for shape in carry_shapes
    ]
    g_shape = (len(todo), 3 * rank, block)
    if todo[-1] == 0:
        out_specs = [pl.BlockSpec((n, slots, piece, per), lambda i: (0, 0, 0, i)), whole(g_shape)]
        out_shape = [(n, slots, piece, heads * per), g_shape]
    else:
        out_specs = [whole(g_shape)] + carry_specs
        out_shape = [g_shape] + carry_shapes
    first_call = todo[0] == blocks - 1
    pairs = sum(b + 1 for b in todo) / (blocks * (blocks + 1) / 2)
    return pl.pallas_call(
        functools.partial(attention_kernel, groups, slots, blocks, todo),
        grid=(heads,),
        in_specs=[
            pl.BlockSpec((rows, wide), lambda i: (0, first + i)),
            pl.BlockSpec((rows, head), lambda i: (0, first + i)),
            pl.BlockSpec((rows, head), lambda i: (0, first + i)),
            pl.BlockSpec((rows, wide), lambda i: (0, first + i)),
        ]
        + [whole((3 * rank, block))] * used
        + [
            pl.BlockSpec((n, slots, piece, per), lambda i: (0, 0, 0, i)),
            whole((1, rows)),
            whole((1, rows)),
            whole((rows, 1)),
            whole(g.shape),
        ]
        + ([] if first_call else carry_specs),
        out_specs=out_specs,
        out_shape=[jax.ShapeDtypeStruct(shape, F32) for shape in out_shape],
        scratch_shapes=[
            pltpu.VMEM((rows, rows), F32),
            pltpu.VMEM((3, used, spans, block), BF16),
            pltpu.VMEM((3, used, spans, block), BF16),
            pltpu.VMEM((3, used * block, spans), BF16),
            pltpu.VMEM((3, used * block, spans), BF16),
            pltpu.VMEM((spans, per), F32),
            pltpu.VMEM((spans, per), F32),
            pltpu.VMEM((rows, head), F32),
            pltpu.VMEM((rows, head), F32),
            pltpu.VMEM((groups * block, head), BF16),
            pltpu.VMEM((groups * block, head), BF16),
            pltpu.VMEM((rows, groups * block), F32),
            pltpu.VMEM((rows, groups * block), F32),
            pltpu.VMEM((rows, groups * block), BF16),
            pltpu.VMEM((rows, groups * block), BF16),
        ],
        cost_estimate=cost(ATTENTION_MICROS * heads * pairs),
        compiler_params=pltpu.CompilerParams(vmem_limit_bytes=VMEM_LIMIT),
        name="attention_grads",
    )(
        fq,
        fk,
        fv,
        up,
        *lows[:used],
        panels,
        slot_rows,
        docs[None, :],
        docs[:, None],
        g,
        *(() if first_call else carry),
    )


def down_grad_kernel(blocks, per_step, order_ref, first_ref, owner_ref, source_ref, *refs):
    x_refs, g_refs = refs[:blocks], refs[blocks : 3 * blocks]
    out_ref, x_all, g_ref, sems = refs[3 * blocks :]
    half = g_refs[0].shape[0]
    step = pl.program_id(0)

    @pl.when(step == 0)
    def _():
        copies = [
            pltpu.make_async_copy(
                x_refs[b].at[:, pl.ds(0, x_all.shape[2])], x_all.at[b], sems.at[b]
            )
            for b in range(blocks)
        ] + [
            pltpu.make_async_copy(
                ref, g_ref.at[i // 2, pl.ds(i % 2 * half, half)], sems.at[blocks + i]
            )
            for i, ref in enumerate(g_refs)
        ]
        for copy in copies:
            copy.start()
        for copy in copies:
            copy.wait()

    out_ref[...] = jnp.zeros_like(out_ref)
    start, stop = first_ref[step * per_step], first_ref[(step + 1) * per_step]
    unroll = 4

    def add(i, carry):
        terms = []
        for u in range(unroll):
            e = start + i * unroll + u
            item = order_ref[jnp.minimum(e, stop - 1)]
            place = item // blocks
            b = item - place * blocks
            x = x_all[b, source_ref[place]].astype(BF16)
            high, low = split2(g_ref[b, place])
            terms.append((e, item, mm(high, x) + mm(low, x)))
        for e, item, term in terms:
            t = owner_ref[item] - step * per_step

            @pl.when(e < stop)
            def _():
                out_ref[t] += term

        return carry

    lax.fori_loop(0, (stop - start + unroll - 1) // unroll, add, 0)


def down_grad(xs, g, owners, source, tenants):
    blocks = len(xs)
    n, rows, width = xs[1].shape
    rank = g[0].shape[1]
    order, first = by_tenant(owners, tenants)
    per_step = 8
    return pl.pallas_call(
        functools.partial(down_grad_kernel, blocks, per_step),
        grid_spec=pltpu.PrefetchScalarGridSpec(
            num_scalar_prefetch=4,
            grid=(tenants // per_step,),
            in_specs=[pl.BlockSpec(memory_space=pl.ANY)] * (3 * blocks),
            out_specs=pl.BlockSpec((per_step, rank, width), lambda i, *_: (i, 0, 0)),
            scratch_shapes=[
                pltpu.VMEM((blocks, n, rows, width), F32),
                pltpu.VMEM((blocks, n) + g[0].shape[1:], F32),
                pltpu.SemaphoreType.DMA((3 * blocks,)),
            ],
        ),
        out_shape=jax.ShapeDtypeStruct((tenants, rank, width), F32),
        compiler_params=pltpu.CompilerParams(vmem_limit_bytes=VMEM_LIMIT),
        cost_estimate=cost(14),
        name="down_grad",
    )(order, first, owners, source, *xs, *g)


def down_grad_last_kernel(owner_ref, leader_ref, source_ref, *refs):
    x_ref, g0_ref, g1_ref, sum_ref, out_ref, x_all, g_all, acc, in_sems, out_sems = refs
    del sum_ref
    n, rows, _ = x_all.shape
    half = n // 2
    loads = [
        pltpu.make_async_copy(x_ref.at[:, pl.ds(0, rows)], x_all, in_sems.at[n]),
        pltpu.make_async_copy(g0_ref, g_all.at[pl.ds(0, half)], in_sems.at[n + 1]),
        pltpu.make_async_copy(g1_ref, g_all.at[pl.ds(half, half)], in_sems.at[n + 2]),
    ]
    for load in loads:
        load.start()

    def tile(p, inward):
        there, here = out_ref.at[owner_ref[p]], acc.at[p]
        if inward:
            return pltpu.make_async_copy(there, here, in_sems.at[p])
        return pltpu.make_async_copy(here, there, out_sems.at[p])

    def leaders(act):
        for p in range(n):
            pl.when(leader_ref[p] == p)(functools.partial(act, p))

    leaders(lambda p: tile(p, True).start())
    for load in loads:
        load.wait()
    leaders(lambda p: tile(p, True).wait())
    for p in range(n):
        x = x_all[source_ref[p]].astype(BF16)
        high, low = split2(g_all[p])
        acc[leader_ref[p]] += mm(high, x) + mm(low, x)
    leaders(lambda p: tile(p, False).start())
    leaders(lambda p: tile(p, False).wait())


def down_grad_last(x, g, total, owner, source):
    n, rank, rows = 2 * g[0].shape[0], g[0].shape[1], g[0].shape[2]
    width = x.shape[2]
    index = jnp.arange(n, dtype=jnp.int32)
    same = owner[None, :] == owner[:, None]
    leader = jnp.min(jnp.where(same, index[None, :], n), axis=1).astype(jnp.int32)
    return pl.pallas_call(
        down_grad_last_kernel,
        grid_spec=pltpu.PrefetchScalarGridSpec(
            num_scalar_prefetch=3,
            grid=(1,),
            in_specs=[pl.BlockSpec(memory_space=pl.ANY)] * 4,
            out_specs=pl.BlockSpec(memory_space=pl.ANY),
            scratch_shapes=[
                pltpu.VMEM((n, rows, width), F32),
                pltpu.VMEM((n, rank, rows), F32),
                pltpu.VMEM((n, rank, width), F32),
                pltpu.SemaphoreType.DMA((n + 3,)),
                pltpu.SemaphoreType.DMA((n,)),
            ],
        ),
        out_shape=jax.ShapeDtypeStruct(total.shape, F32),
        input_output_aliases={6: 0},
        cost_estimate=cost(6),
        compiler_params=pltpu.CompilerParams(vmem_limit_bytes=VMEM_LIMIT),
        name="down_grad_last",
    )(owner, leader, source, x, *g, total)


def up_grad_kernel(calls, per_step, kv_heads, head, order_ref, first_ref, *refs):
    in_refs, (q_ref, kv_ref, kv_sum) = refs[:calls], refs[calls:]
    step = pl.program_id(0)
    wide = q_ref.shape[2] // kv_heads
    per = wide + 2 * head
    heads = kv_heads // calls
    for t in range(per_step):
        tenant = step * per_step + t
        q_ref[t] = jnp.zeros(q_ref.shape[1:], F32)
        kv_sum[...] = jnp.zeros_like(kv_sum)

        def add(e, carry):
            item = order_ref[e]
            for c in range(calls):
                for h in range(heads):
                    at = c * heads + h
                    q_ref[t, :, at * wide : (at + 1) * wide] += in_refs[c][
                        item, :, h * per : h * per + wide
                    ]
                    kv_sum[at] += in_refs[c][item, :, h * per + wide : (h + 1) * per]
            return carry

        lax.fori_loop(first_ref[tenant], first_ref[tenant + 1], add, 0)
        for k in range(kv_ref.shape[1]):
            for h in range(kv_heads):
                kv_ref[t, k, h, :] = kv_sum[h, k, :]


def up_grad(dus, order, first, tenants, kv_heads, head):
    calls = len(dus)
    items, piece, cols = dus[0].shape
    per_step = 8
    wide = cols * calls // kv_heads - 2 * head
    return pl.pallas_call(
        functools.partial(up_grad_kernel, calls, per_step, kv_heads, head),
        grid_spec=pltpu.PrefetchScalarGridSpec(
            num_scalar_prefetch=2,
            grid=(tenants // per_step,),
            in_specs=[pl.BlockSpec((items, piece, cols), lambda i, *_: (0, 0, 0))] * calls,
            out_specs=[
                pl.BlockSpec((per_step, piece, kv_heads * wide), lambda i, *_: (i, 0, 0)),
                pl.BlockSpec((per_step, piece, kv_heads, 2 * head), lambda i, *_: (i, 0, 0, 0)),
            ],
            scratch_shapes=[pltpu.VMEM((kv_heads, piece, 2 * head), F32)],
        ),
        out_shape=[
            jax.ShapeDtypeStruct((tenants, piece, kv_heads * wide), F32),
            jax.ShapeDtypeStruct((tenants, piece, kv_heads, 2 * head), F32),
        ],
        compiler_params=pltpu.CompilerParams(vmem_limit_bytes=VMEM_LIMIT),
        cost_estimate=cost(6),
        name="up_grad",
    )(order, first, *dus)


def exchange(a):
    return lax.all_to_all(a, "dp", split_axis=0, concat_axis=0, tiled=True)


def on_device(
    dp_count,
    mp_count,
    normed_input_rows,
    frozen_queries,
    frozen_keys,
    frozen_values,
    attention_output_gradient,
    adapter_down_weight,
    adapter_up_query,
    adapter_up_key_value,
    document_numbers,
    block_tenant_slot,
    shard_tenant_table,
):
    rows = normed_input_rows.shape[0]
    blocks = block_tenant_slot.shape[0]
    block = rows // blocks
    tenants, width, ranks = adapter_down_weight.shape
    slots = shard_tenant_table.shape[1]
    piece = adapter_up_query.shape[1]
    kv_heads = adapter_up_key_value.shape[2]
    head = adapter_up_key_value.shape[3] // 2
    wide = adapter_up_query.shape[2] // kv_heads
    me = lax.axis_index("dp").astype(jnp.int32)

    wires = [
        rows_wire(normed_input_rows, block_tenant_slot, dp_count, b) for b in range(blocks)
    ]
    wanted = shard_tenant_table.reshape(-1)
    up_query = adapter_up_query[wanted].reshape(-1, piece, kv_heads, wide)
    up_key_value = adapter_up_key_value[wanted]
    wire = jnp.concatenate([up_query, up_key_value], axis=-1)
    heads = min(HEADS_PER_CALL, kv_heads)
    calls = kv_heads // heads
    per = wide + 2 * head
    owns = [
        wire[:, :, c * heads : (c + 1) * heads].reshape(-1, piece, heads * per)
        for c in range(calls)
    ]

    xs = [exchange(wires[0])]
    for b in range(1, blocks):
        xs.append(exchange(after(wires[b], xs[-1], *(owns if b == blocks - 1 else ()))))

    source = me ^ bit_reverse(
        jnp.arange(dp_count, dtype=jnp.int32), dp_count.bit_length() - 1
    )
    slots_all = xs[0][:, block, :blocks].astype(jnp.int32)[source]
    owners = shard_tenant_table[source[:, None], slots_all]

    weights = jnp.swapaxes(adapter_down_weight, 1, 2)
    part = down_partial(xs[:-1], weights, source, owners[:, :-1], block)
    near = scatter_near(part, "dp", dp_count)
    early = sum_over(scatter_far(near, "dp", dp_count), "mp", mp_count)
    part = down_partial(xs[-1:], weights, source, owners[:, -1:], block)
    late_part = scatter_far(scatter_near(part, "dp", dp_count), "dp", dp_count)
    late = sum_over(late_part, "mp", mp_count)
    lows = [early[b] for b in range(blocks - 1)] + [late[0]]

    panels = []
    for c in range(calls):
        own = after(owns[c], xs[-1], near) if c == 0 else after(owns[c], panels[-1], late_part)
        panels.append(exchange(own).reshape(dp_count, slots, piece, heads * per))

    attend = functools.partial(
        attention,
        frozen_queries,
        frozen_keys,
        frozen_values,
        attention_output_gradient,
        lows,
        slot_rows=jnp.repeat(block_tenant_slot, block)[None, :],
        docs=document_numbers,
        head=head,
        heads=heads,
    )
    g = jnp.zeros((blocks, 3 * piece * dp_count, block), F32)
    every = tuple(range(blocks))[::-1]
    dus = []
    for c in range(calls - 1):
        du, g = attend(panels=panels[c], g=g, first=c * heads, todo=every, carry=())
        dus.append(exchange(du.reshape(dp_count * slots, piece, heads * per)))
    sums, fars, carry = {}, {}, ()
    for b in every:
        if b == blocks - 3:
            fars[blocks - 1] = gather_far(sums[blocks - 1], "dp", dp_count)
            carry = after(carry, sums[blocks - 1])
        out = attend(panels=panels[-1], g=g, first=kv_heads - heads, todo=(b,), carry=carry)
        du, g_b = out if b == 0 else (None, out[0])
        carry = out[1:]
        if b == 0:
            g_b = after(g_b, *dus, fars[blocks - 1], *(sums[k] for k in every[:-1]))
        sums[b] = sum_over(g_b, "mp", mp_count)
    du = du.reshape(dp_count * slots, piece, heads * per)
    g_halves = [None] * blocks
    for b in every:
        if b not in fars:
            fars[b] = gather_far(sums[b], "dp", dp_count)
        fars[b] = gather_step(fars[b], "dp", dp_count, 2)
        if b > 0:
            g_halves[b] = (fars[b], swap(fars[b], "dp", dp_count, 1))
    dus.append(exchange(du))

    early = [half for pair in g_halves[1:] for half in pair]
    grad_down = down_grad(xs[1:], early, owners[:, 1:].reshape(-1), source, tenants)
    fars[0] = after(fars[0], grad_down)
    g_halves[0] = (fars[0], swap(fars[0], "dp", dp_count, 1))
    grad_down = down_grad_last(xs[0], g_halves[0], grad_down, owners[:, 0], source)
    order, first = by_tenant(wanted, tenants)
    grad_upq, grad_upkv = up_grad(dus, order, first, tenants, kv_heads, head)
    return (
        jnp.swapaxes(grad_down, 1, 2),
        grad_upq,
        grad_upkv,
    )


def solution(mesh):
    placed = (
        P("dp", "mp"),
        P("dp", "mp"),
        P("dp", "mp"),
        P("dp", "mp"),
        P("dp", "mp"),
        P(None, ("mp", "dp"), None),
        P(None, "dp", "mp"),
        P(None, "dp", "mp", None),
        P("dp"),
        P("dp"),
        P(),
    )
    return jax.shard_map(
        functools.partial(on_device, mesh.shape["dp"], mesh.shape["mp"]),
        mesh=mesh,
        in_specs=placed,
        out_specs=(P(None, ("mp", "dp"), None), P(None, "dp", "mp"), P(None, "dp", "mp", None)),
        check_vma=False,
    )
```

```python
import functools

import jax
import jax.numpy as jnp
from jax import lax
from jax.experimental import pallas as pl
from jax.experimental.pallas import tpu as pltpu
from jax.sharding import PartitionSpec as P

ADAPTER_SCALE = 0.5
MASKED = -1e30
BF16, F32 = jnp.bfloat16, jnp.float32
VMEM_LIMIT = 56 * 1024 * 1024
NN = (((1,), (0,)), ((), ()))
NT = (((1,), (1,)), ((), ()))
TN = (((0,), (0,)), ((), ()))
HEADS_PER_CALL = 2
ATTENTION_MICROS = 10
DOWN_MICROS = 2


def cost(micros):
    return pl.CostEstimate(
        flops=int(micros * 1e9), bytes_accessed=int(micros * 3.6e6), transcendentals=0
    )


def split2(a):
    high = a.astype(BF16)
    return high, (a - high.astype(F32)).astype(BF16)


def mm(a, b, dims=NN):
    return lax.dot_general(a, b, dims, preferred_element_type=F32)


def mm3(a, b, dims=NN):
    (ah, al), (bh, bl) = a, b
    return mm(ah, bh, dims) + mm(ah, bl, dims) + mm(al, bh, dims)


def bit_reverse(value, bits):
    out = jnp.zeros_like(value)
    for k in range(bits):
        out = out | (((value >> k) & 1) << (bits - 1 - k))
    return out


def swap(a, axis, size, bit):
    return lax.ppermute(a, axis, [(i, i ^ bit) for i in range(size)])


def sum_over(a, axis, size):
    bit = 1
    while bit < size:
        a = a + swap(a, axis, size, bit)
        bit *= 2
    return a


def scatter_near(part, axis, size):
    bit = 1
    while bit < min(size, 4):
        half = part.shape[0] // 2
        part = part[:half] + swap(part[half:], axis, size, bit)
        bit *= 2
    return part


def scatter_far(part, axis, size):
    bit = min(size, 4)
    moved = [
        swap(part[k], axis, size, bit_reversed(k, part.shape[0]) * bit)
        for k in range(1, part.shape[0])
    ]
    return functools.reduce(jnp.add, moved, part[0])


def bit_reversed(k, size):
    out = 0
    for i in range(size.bit_length() - 1):
        out |= (k >> i & 1) << (size.bit_length() - 2 - i)
    return out


def gather_far(a, axis, size):
    far = max(size // 4, 1)
    moved = [a] + [swap(a, axis, size, bit_reversed(k, far) * 4) for k in range(1, far)]
    return jnp.concatenate(moved, axis=0)


def gather_step(a, axis, size, bit):
    return jnp.concatenate([a, swap(a, axis, size, bit)], axis=0)


def after(a, *others):
    return lax.optimization_barrier((a,) + others)[0]


def by_tenant(owners, tenants):
    count = owners.shape[0]
    index = jnp.arange(count, dtype=jnp.int32)
    ahead = (owners[None, :] < owners[:, None]) | (
        (owners[None, :] == owners[:, None]) & (index[None, :] < index[:, None])
    )
    place = jnp.sum(ahead.astype(jnp.int32), axis=1)
    order = jnp.sum(
        jnp.where(place[None, :] == index[:, None], index[None, :], 0), axis=1
    )
    edge = jnp.arange(tenants + 1, dtype=jnp.int32)
    first = jnp.sum((owners[None, :] < edge[:, None]).astype(jnp.int32), axis=1)
    return order.astype(jnp.int32), first.astype(jnp.int32)


def wire_kernel(n, slot_ref, x_ref, out_ref):
    rows = x_ref.shape[0]
    width = x_ref.shape[1] // n
    for r in range(n):
        out_ref[r, :rows] = x_ref[:, r * width : (r + 1) * width].astype(F32)
    if out_ref.shape[1] > rows:
        lane = lax.broadcasted_iota(jnp.int32, (8, width), 1)
        tile = jnp.zeros((8, width), F32)
        for b in range(slot_ref.shape[0]):
            tile = jnp.where(lane == b, slot_ref[b].astype(F32), tile)
        out_ref[:, rows:] = jnp.broadcast_to(tile[None], (n, 8, width))


def rows_wire(x, block_slots, n, start, rows):
    width = x.shape[1] // n
    per = min(n, max(128 // width, 1) * 4)
    tall = rows + (8 if start == 0 else 0)
    return pl.pallas_call(
        functools.partial(wire_kernel, per),
        grid_spec=pltpu.PrefetchScalarGridSpec(
            num_scalar_prefetch=1,
            grid=(n // per,),
            in_specs=[pl.BlockSpec((rows, per * width), lambda i, s: (start // rows, i))],
            out_specs=pl.BlockSpec((per, tall, width), lambda i, s: (i, 0, 0)),
        ),
        out_shape=jax.ShapeDtypeStruct((n, tall, width), F32),
        cost_estimate=cost(2),
        compiler_params=pltpu.CompilerParams(vmem_limit_bytes=VMEM_LIMIT),
        name="rows_wire",
    )(block_slots, x)


def down_kernel(count, calls, source_ref, tenant_ref, *refs):
    x_refs, w_refs, out_ref = refs[: count * calls], refs[count * calls : -1], refs[-1]
    for c in range(count):
        for b in range(calls):
            x = x_refs[c * calls + b][0].astype(BF16)
            high, low = split2(w_refs[c * calls + b][0])
            out_ref[c, b] = mm(high, x, NT) + mm(low, x, NT)


def down_partial(xs, weights, source, tenant, rows):
    n, _, width = xs[0][0].shape
    rank = weights.shape[1]
    calls = len(xs)
    count = 4 // calls
    every = [(c, b) for c in range(count) for b in range(calls)]

    def x_spec(c, b):
        return pl.BlockSpec((1, rows, width), lambda p, s, t: (s[p * count + c], xs[b][1] // rows, 0))

    def w_spec(c, b):
        return pl.BlockSpec(
            (1, rank, width), lambda p, s, t: (t[(p * count + c) * calls + b], 0, 0)
        )

    return pl.pallas_call(
        functools.partial(down_kernel, count, calls),
        grid_spec=pltpu.PrefetchScalarGridSpec(
            num_scalar_prefetch=2,
            grid=(n // count,),
            in_specs=[x_spec(*at) for at in every] + [w_spec(*at) for at in every],
            out_specs=pl.BlockSpec((count, calls, rank, rows), lambda p, s, t: (p, 0, 0, 0)),
        ),
        out_shape=jax.ShapeDtypeStruct((n, calls, rank, rows), F32),
        cost_estimate=cost(DOWN_MICROS * calls),
        compiler_params=pltpu.CompilerParams(vmem_limit_bytes=VMEM_LIMIT),
        name="down_partial",
    )(source, tenant.reshape(-1), *[xs[b][0] for _, b in every], *[weights] * len(every))


def attention_kernel(groups, slots, blocks, todo, *refs):
    first_call, last_call = todo[0] == blocks - 1, todo[-1] == 0
    used = todo[0] + 1
    fq_ref, fk_ref, fv_ref, up_ref = refs[:4]
    low_refs = refs[4 : 4 + used]
    panel_ref, slot_ref, doc_row_ref, doc_col_ref, g_in_ref = refs[4 + used : 9 + used]
    refs = refs[9 + used :]
    if not first_call:
        carry_in, refs = refs[:3], refs[3:]
    if last_call:
        (du_ref, g_ref), refs = refs[:2], refs[2:]
    else:
        (g_ref, *carry_out), refs = refs[:4], refs[4:]
    bias, lct_h, lct_l, lc_h, lc_l, panel, du, dk, dv, q_s, up_s, sc, gp, ds, pr = refs
    step = pl.program_id(0)
    rows, head = fk_ref.shape
    block = rows // blocks
    owners, _, piece, _ = panel_ref.shape
    rank = owners * piece
    wide = groups * head
    inverse = 1.0 / head**0.5
    slot = slot_ref[...]

    @pl.when(step == 0)
    def _():
        key = lax.broadcasted_iota(jnp.int32, (rows, rows), 0)
        row = lax.broadcasted_iota(jnp.int32, (rows, rows), 1)
        joined = (doc_row_ref[...] == doc_col_ref[...]) & (row >= key)
        bias[...] = jnp.where(joined, 0.0, MASKED)
        for b in range(used):
            span = slice(b * block, (b + 1) * block)
            for part in range(3):
                low = low_refs[b][part * rank : (part + 1) * rank, :] * ADAPTER_SCALE
                both = jnp.concatenate(
                    [jnp.where(slot[:, span] == s, low, 0.0) for s in range(slots)], axis=0
                )
                lct_h[part, b], lct_l[part, b] = split2(both)
                lc_h[part, span, :], lc_l[part, span, :] = split2(both.T)
        for b in todo:
            g_ref[b - todo[-1]] = g_in_ref[b] * (1.0 / ADAPTER_SCALE)

    for w in range(owners):
        for s in range(slots):
            start = s * rank + w * piece
            panel[start : start + piece, :] = panel_ref[w, s]
    u_q = split2(panel[:, :wide])
    u_k = split2(panel[:, wide : wide + head])
    u_v = split2(panel[:, wide + head :])
    seen = used * block
    k = fk_ref[:seen].astype(F32) + mm3((lc_h[1, :seen], lc_l[1, :seen]), u_k)
    v = fv_ref[:seen].astype(F32) + mm3((lc_h[2, :seen], lc_l[2, :seen]), u_v)
    k, v = k.astype(BF16), v.astype(BF16)
    k_t = k.T
    if first_call:
        dk[...] = jnp.zeros_like(dk)
        dv[...] = jnp.zeros_like(dv)
        du[...] = jnp.zeros_like(du)
    else:
        dk[...], dv[...], du[...] = [ref[0] for ref in carry_in]

    for b in todo:
        here = slice(b * block, (b + 1) * block)
        reach = (b + 1) * block
        q = fq_ref[here].astype(F32) + mm3((lc_h[0, here], lc_l[0, here]), u_q)
        q = q.astype(BF16)
        for h in range(groups):
            at, lanes = slice(h * block, (h + 1) * block), slice(h * head, (h + 1) * head)
            q_s[at] = q[:, lanes]
            up_s[at] = up_ref[here, lanes]
        sc[:reach] = mm(k[:reach], q_s[...], NT)
        gp[:reach] = mm(v[:reach], up_s[...], NT)
        mask = bias[:reach, here]
        for h in range(groups):
            at = slice(h * block, (h + 1) * block)
            scores = sc[:reach, at] * inverse + mask
            weights = jnp.exp(scores - jnp.max(scores, axis=0, keepdims=True))
            scale = 1.0 / jnp.sum(weights, axis=0, keepdims=True)
            grad_probs = gp[:reach, at]
            probs = weights * scale
            inner = jnp.sum(probs * grad_probs, axis=0, keepdims=True)
            ds[:reach, at] = (probs * (grad_probs - inner) * inverse).astype(BF16)
            pr[:reach, at] = probs.astype(BF16)
        dk[:reach] += mm(ds[:reach], q_s[...])
        dv[:reach] += mm(pr[:reach], up_s[...])
        dq = mm(k_t[:, :reach], ds[:reach]).astype(BF16)
        dk_b, dv_b = split2(dk[here]), split2(dv[here])
        lct = [(lct_h[part, b], lct_l[part, b]) for part in range(3)]
        both = jnp.zeros((slots * rank, block), F32)
        for h in range(groups):
            at, lanes = slice(h * block, (h + 1) * block), slice(h * head, (h + 1) * head)
            du[:, lanes] += mm(lct[0][0], dq[:, at], NT)
            both += mm(u_q[0][:, lanes], dq[:, at])
        du[:, wide : wide + head] += mm3(lct[1], dk_b)
        du[:, wide + head :] += mm3(lct[2], dv_b)
        for part, full in enumerate((both, mm3(u_k, dk_b, NT), mm3(u_v, dv_b, NT))):
            mine = jnp.zeros((rank, block), F32)
            for s in range(slots):
                mine += jnp.where(slot[:, here] == s, full[s * rank : (s + 1) * rank], 0.0)
            g_ref[b - todo[-1], part * rank : (part + 1) * rank, :] += mine

    @pl.when(step == pl.num_programs(0) - 1)
    def _():
        g_ref[...] *= ADAPTER_SCALE

    if last_call:
        for w in range(owners):
            for s in range(slots):
                start = s * rank + w * piece
                du_ref[w, s] = du[start : start + piece, :]
    else:
        for ref, value in zip(carry_out, (dk, dv, du)):
            ref[0] = value[...]


def attention(
    fq, fk, fv, up, lows, *, panels, slot_rows, docs, g, head, first, heads, todo, carry
):
    rows = fq.shape[0]
    blocks = len(lows)
    block = rows // blocks
    n, slots, piece, cols = panels.shape
    kv_heads = fk.shape[1] // head
    groups = fq.shape[1] // fk.shape[1]
    wide = groups * head
    per = wide + 2 * head
    rank = n * piece
    spans = slots * rank
    used = todo[0] + 1
    whole = lambda shape: pl.BlockSpec(shape, lambda i: (0,) * len(shape))
    carry_shapes = [(heads, rows, head), (heads, rows, head), (heads, spans, per)]
    carry_specs = [
        pl.BlockSpec((1,) + shape[1:], lambda i: (i, 0, 0)) for shape in carry_shapes
    ]
    g_shape = (len(todo), 3 * rank, block)
    if todo[-1] == 0:
        out_specs = [pl.BlockSpec((n, slots, piece, per), lambda i: (0, 0, 0, i)), whole(g_shape)]
        out_shape = [(n, slots, piece, heads * per), g_shape]
    else:
        out_specs = [whole(g_shape)] + carry_specs
        out_shape = [g_shape] + carry_shapes
    first_call = todo[0] == blocks - 1
    pairs = sum(b + 1 for b in todo) / (blocks * (blocks + 1) / 2)
    return pl.pallas_call(
        functools.partial(attention_kernel, groups, slots, blocks, todo),
        grid=(heads,),
        in_specs=[
            pl.BlockSpec((rows, wide), lambda i: (0, first + i)),
            pl.BlockSpec((rows, head), lambda i: (0, first + i)),
            pl.BlockSpec((rows, head), lambda i: (0, first + i)),
            pl.BlockSpec((rows, wide), lambda i: (0, first + i)),
        ]
        + [whole((3 * rank, block))] * used
        + [
            pl.BlockSpec((n, slots, piece, per), lambda i: (0, 0, 0, i)),
            whole((1, rows)),
            whole((1, rows)),
            whole((rows, 1)),
            whole(g.shape),
        ]
        + ([] if first_call else carry_specs),
        out_specs=out_specs,
        out_shape=[jax.ShapeDtypeStruct(shape, F32) for shape in out_shape],
        scratch_shapes=[
            pltpu.VMEM((rows, rows), F32),
            pltpu.VMEM((3, used, spans, block), BF16),
            pltpu.VMEM((3, used, spans, block), BF16),
            pltpu.VMEM((3, used * block, spans), BF16),
            pltpu.VMEM((3, used * block, spans), BF16),
            pltpu.VMEM((spans, per), F32),
            pltpu.VMEM((spans, per), F32),
            pltpu.VMEM((rows, head), F32),
            pltpu.VMEM((rows, head), F32),
            pltpu.VMEM((groups * block, head), BF16),
            pltpu.VMEM((groups * block, head), BF16),
            pltpu.VMEM((rows, groups * block), F32),
            pltpu.VMEM((rows, groups * block), F32),
            pltpu.VMEM((rows, groups * block), BF16),
            pltpu.VMEM((rows, groups * block), BF16),
        ],
        cost_estimate=cost(ATTENTION_MICROS * heads * pairs),
        compiler_params=pltpu.CompilerParams(vmem_limit_bytes=VMEM_LIMIT),
        name="attention_grads",
    )(
        fq,
        fk,
        fv,
        up,
        *lows[:used],
        panels,
        slot_rows,
        docs[None, :],
        docs[:, None],
        g,
        *(() if first_call else carry),
    )


def down_grad_kernel(starts, per_step, order_ref, first_ref, owner_ref, source_ref, *refs):
    blocks = len(starts)
    x_refs, g_refs = refs[:blocks], refs[blocks : 3 * blocks]
    out_ref, x_all, g_ref, sems = refs[3 * blocks :]
    half = g_refs[0].shape[0]
    step = pl.program_id(0)

    @pl.when(step == 0)
    def _():
        copies = [
            pltpu.make_async_copy(
                x_refs[b].at[:, pl.ds(starts[b], x_all.shape[2])], x_all.at[b], sems.at[b]
            )
            for b in range(blocks)
        ] + [
            pltpu.make_async_copy(
                ref, g_ref.at[i // 2, pl.ds(i % 2 * half, half)], sems.at[blocks + i]
            )
            for i, ref in enumerate(g_refs)
        ]
        for copy in copies:
            copy.start()
        for copy in copies:
            copy.wait()

    out_ref[...] = jnp.zeros_like(out_ref)
    start, stop = first_ref[step * per_step], first_ref[(step + 1) * per_step]
    unroll = 4

    def add(i, carry):
        terms = []
        for u in range(unroll):
            e = start + i * unroll + u
            item = order_ref[jnp.minimum(e, stop - 1)]
            place = item // blocks
            b = item - place * blocks
            x = x_all[b, source_ref[place]].astype(BF16)
            high, low = split2(g_ref[b, place])
            terms.append((e, item, mm(high, x) + mm(low, x)))
        for e, item, term in terms:
            t = owner_ref[item] - step * per_step

            @pl.when(e < stop)
            def _():
                out_ref[t] += term

        return carry

    lax.fori_loop(0, (stop - start + unroll - 1) // unroll, add, 0)


def down_grad(xs, g, owners, source, tenants):
    blocks = len(xs)
    n, _, width = xs[0][0].shape
    rows = g[0].shape[2]
    rank = g[0].shape[1]
    order, first = by_tenant(owners, tenants)
    per_step = 8
    return pl.pallas_call(
        functools.partial(down_grad_kernel, [start for _, start in xs], per_step),
        grid_spec=pltpu.PrefetchScalarGridSpec(
            num_scalar_prefetch=4,
            grid=(tenants // per_step,),
            in_specs=[pl.BlockSpec(memory_space=pl.ANY)] * (3 * blocks),
            out_specs=pl.BlockSpec((per_step, rank, width), lambda i, *_: (i, 0, 0)),
            scratch_shapes=[
                pltpu.VMEM((blocks, n, rows, width), F32),
                pltpu.VMEM((blocks, n) + g[0].shape[1:], F32),
                pltpu.SemaphoreType.DMA((3 * blocks,)),
            ],
        ),
        out_shape=jax.ShapeDtypeStruct((tenants, rank, width), F32),
        compiler_params=pltpu.CompilerParams(vmem_limit_bytes=VMEM_LIMIT),
        cost_estimate=cost(14),
        name="down_grad",
    )(order, first, owners, source, *[x for x, _ in xs], *g)


def down_grad_last_kernel(owner_ref, leader_ref, source_ref, *refs):
    x_ref, g0_ref, g1_ref, sum_ref, out_ref, x_all, g_all, acc, in_sems, out_sems = refs
    del sum_ref
    n, rows, _ = x_all.shape
    half = n // 2
    loads = [
        pltpu.make_async_copy(x_ref.at[:, pl.ds(0, rows)], x_all, in_sems.at[n]),
        pltpu.make_async_copy(g0_ref, g_all.at[pl.ds(0, half)], in_sems.at[n + 1]),
        pltpu.make_async_copy(g1_ref, g_all.at[pl.ds(half, half)], in_sems.at[n + 2]),
    ]
    for load in loads:
        load.start()

    def tile(p, inward):
        there, here = out_ref.at[owner_ref[p]], acc.at[p]
        if inward:
            return pltpu.make_async_copy(there, here, in_sems.at[p])
        return pltpu.make_async_copy(here, there, out_sems.at[p])

    def leaders(act):
        for p in range(n):
            pl.when(leader_ref[p] == p)(functools.partial(act, p))

    leaders(lambda p: tile(p, True).start())
    for load in loads:
        load.wait()
    leaders(lambda p: tile(p, True).wait())
    for p in range(n):
        x = x_all[source_ref[p]].astype(BF16)
        high, low = split2(g_all[p])
        acc[leader_ref[p]] += mm(high, x) + mm(low, x)
    leaders(lambda p: tile(p, False).start())
    leaders(lambda p: tile(p, False).wait())


def down_grad_last(x, g, total, owner, source):
    n, rank, rows = 2 * g[0].shape[0], g[0].shape[1], g[0].shape[2]
    width = x.shape[2]
    index = jnp.arange(n, dtype=jnp.int32)
    same = owner[None, :] == owner[:, None]
    leader = jnp.min(jnp.where(same, index[None, :], n), axis=1).astype(jnp.int32)
    return pl.pallas_call(
        down_grad_last_kernel,
        grid_spec=pltpu.PrefetchScalarGridSpec(
            num_scalar_prefetch=3,
            grid=(1,),
            in_specs=[pl.BlockSpec(memory_space=pl.ANY)] * 4,
            out_specs=pl.BlockSpec(memory_space=pl.ANY),
            scratch_shapes=[
                pltpu.VMEM((n, rows, width), F32),
                pltpu.VMEM((n, rank, rows), F32),
                pltpu.VMEM((n, rank, width), F32),
                pltpu.SemaphoreType.DMA((n + 3,)),
                pltpu.SemaphoreType.DMA((n,)),
            ],
        ),
        out_shape=jax.ShapeDtypeStruct(total.shape, F32),
        input_output_aliases={6: 0},
        cost_estimate=cost(6),
        compiler_params=pltpu.CompilerParams(vmem_limit_bytes=VMEM_LIMIT),
        name="down_grad_last",
    )(owner, leader, source, x, *g, total)


def up_grad_kernel(calls, per_step, kv_heads, head, order_ref, first_ref, *refs):
    in_refs, (q_ref, kv_ref, kv_sum) = refs[:calls], refs[calls:]
    step = pl.program_id(0)
    wide = q_ref.shape[2] // kv_heads
    per = wide + 2 * head
    heads = kv_heads // calls
    for t in range(per_step):
        tenant = step * per_step + t
        q_ref[t] = jnp.zeros(q_ref.shape[1:], F32)
        kv_sum[...] = jnp.zeros_like(kv_sum)

        def add(e, carry):
            item = order_ref[e]
            for c in range(calls):
                for h in range(heads):
                    at = c * heads + h
                    q_ref[t, :, at * wide : (at + 1) * wide] += in_refs[c][
                        item, :, h * per : h * per + wide
                    ]
                    kv_sum[at] += in_refs[c][item, :, h * per + wide : (h + 1) * per]
            return carry

        lax.fori_loop(first_ref[tenant], first_ref[tenant + 1], add, 0)
        for k in range(kv_ref.shape[1]):
            for h in range(kv_heads):
                kv_ref[t, k, h, :] = kv_sum[h, k, :]


def up_grad(dus, order, first, tenants, kv_heads, head):
    calls = len(dus)
    items, piece, cols = dus[0].shape
    per_step = 8
    wide = cols * calls // kv_heads - 2 * head
    return pl.pallas_call(
        functools.partial(up_grad_kernel, calls, per_step, kv_heads, head),
        grid_spec=pltpu.PrefetchScalarGridSpec(
            num_scalar_prefetch=2,
            grid=(tenants // per_step,),
            in_specs=[pl.BlockSpec((items, piece, cols), lambda i, *_: (0, 0, 0))] * calls,
            out_specs=[
                pl.BlockSpec((per_step, piece, kv_heads * wide), lambda i, *_: (i, 0, 0)),
                pl.BlockSpec((per_step, piece, kv_heads, 2 * head), lambda i, *_: (i, 0, 0, 0)),
            ],
            scratch_shapes=[pltpu.VMEM((kv_heads, piece, 2 * head), F32)],
        ),
        out_shape=[
            jax.ShapeDtypeStruct((tenants, piece, kv_heads * wide), F32),
            jax.ShapeDtypeStruct((tenants, piece, kv_heads, 2 * head), F32),
        ],
        compiler_params=pltpu.CompilerParams(vmem_limit_bytes=VMEM_LIMIT),
        cost_estimate=cost(6),
        name="up_grad",
    )(order, first, *dus)


def exchange(a):
    return lax.all_to_all(a, "dp", split_axis=0, concat_axis=0, tiled=True)


def on_device(
    dp_count,
    mp_count,
    normed_input_rows,
    frozen_queries,
    frozen_keys,
    frozen_values,
    attention_output_gradient,
    adapter_down_weight,
    adapter_up_query,
    adapter_up_key_value,
    document_numbers,
    block_tenant_slot,
    shard_tenant_table,
):
    rows = normed_input_rows.shape[0]
    blocks = block_tenant_slot.shape[0]
    block = rows // blocks
    tenants, width, ranks = adapter_down_weight.shape
    slots = shard_tenant_table.shape[1]
    piece = adapter_up_query.shape[1]
    kv_heads = adapter_up_key_value.shape[2]
    head = adapter_up_key_value.shape[3] // 2
    wide = adapter_up_query.shape[2] // kv_heads
    me = lax.axis_index("dp").astype(jnp.int32)

    early_rows = (blocks - 1) * block
    wires = [
        rows_wire(normed_input_rows, block_tenant_slot, dp_count, start, size)
        for start, size in ((0, early_rows), (early_rows, block))
    ]
    wanted = shard_tenant_table.reshape(-1)
    up_query = adapter_up_query[wanted].reshape(-1, piece, kv_heads, wide)
    up_key_value = adapter_up_key_value[wanted]
    wire = jnp.concatenate([up_query, up_key_value], axis=-1)
    heads = min(HEADS_PER_CALL, kv_heads)
    calls = kv_heads // heads
    per = wide + 2 * head
    owns = [
        wire[:, :, c * heads : (c + 1) * heads].reshape(-1, piece, heads * per)
        for c in range(calls)
    ]

    moved = exchange(wires[0])
    x_last = exchange(after(wires[1], moved, *owns))
    xs = [(moved, b * block) for b in range(blocks - 1)] + [(x_last, 0)]

    source = me ^ bit_reverse(
        jnp.arange(dp_count, dtype=jnp.int32), dp_count.bit_length() - 1
    )
    slots_all = moved[:, early_rows, :blocks].astype(jnp.int32)[source]
    owners = shard_tenant_table[source[:, None], slots_all]

    weights = jnp.swapaxes(adapter_down_weight, 1, 2)
    part = down_partial(xs[:-1], weights, source, owners[:, :-1], block)
    near = scatter_near(part, "dp", dp_count)
    early = sum_over(scatter_far(near, "dp", dp_count), "mp", mp_count)
    part = down_partial(xs[-1:], weights, source, owners[:, -1:], block)
    late_part = scatter_far(scatter_near(part, "dp", dp_count), "dp", dp_count)
    late = sum_over(late_part, "mp", mp_count)
    lows = [early[b] for b in range(blocks - 1)] + [late[0]]

    panels = []
    for c in range(calls):
        own = after(owns[c], x_last, near) if c == 0 else after(owns[c], panels[-1], late_part)
        panels.append(exchange(own).reshape(dp_count, slots, piece, heads * per))

    attend = functools.partial(
        attention,
        frozen_queries,
        frozen_keys,
        frozen_values,
        attention_output_gradient,
        lows,
        slot_rows=jnp.repeat(block_tenant_slot, block)[None, :],
        docs=document_numbers,
        head=head,
        heads=heads,
    )
    g = jnp.zeros((blocks, 3 * piece * dp_count, block), F32)
    every = tuple(range(blocks))[::-1]
    dus = []
    for c in range(calls - 1):
        du, g = attend(panels=panels[c], g=g, first=c * heads, todo=every, carry=())
        dus.append(exchange(du.reshape(dp_count * slots, piece, heads * per)))
    sums, fars, carry = {}, {}, ()
    for b in every:
        if b == blocks - 3:
            fars[blocks - 1] = gather_far(sums[blocks - 1], "dp", dp_count)
            carry = after(carry, sums[blocks - 1])
        out = attend(panels=panels[-1], g=g, first=kv_heads - heads, todo=(b,), carry=carry)
        du, g_b = out if b == 0 else (None, out[0])
        carry = out[1:]
        if b == 0:
            g_b = after(g_b, *dus, fars[blocks - 1], *(sums[k] for k in every[:-1]))
        sums[b] = sum_over(g_b, "mp", mp_count)
    du = du.reshape(dp_count * slots, piece, heads * per)
    g_halves = [None] * blocks
    for b in every:
        if b not in fars:
            fars[b] = gather_far(sums[b], "dp", dp_count)
        fars[b] = gather_step(fars[b], "dp", dp_count, 2)
        if b > 0:
            g_halves[b] = (fars[b], swap(fars[b], "dp", dp_count, 1))
    dus.append(exchange(du))

    early = [half for pair in g_halves[1:] for half in pair]
    grad_down = down_grad(xs[1:], early, owners[:, 1:].reshape(-1), source, tenants)
    fars[0] = after(fars[0], grad_down)
    g_halves[0] = (fars[0], swap(fars[0], "dp", dp_count, 1))
    grad_down = down_grad_last(moved, g_halves[0], grad_down, owners[:, 0], source)
    order, first = by_tenant(wanted, tenants)
    grad_upq, grad_upkv = up_grad(dus, order, first, tenants, kv_heads, head)
    return (
        jnp.swapaxes(grad_down, 1, 2),
        grad_upq,
        grad_upkv,
    )


def solution(mesh):
    placed = (
        P("dp", "mp"),
        P("dp", "mp"),
        P("dp", "mp"),
        P("dp", "mp"),
        P("dp", "mp"),
        P(None, ("mp", "dp"), None),
        P(None, "dp", "mp"),
        P(None, "dp", "mp", None),
        P("dp"),
        P("dp"),
        P(),
    )
    return jax.shard_map(
        functools.partial(on_device, mesh.shape["dp"], mesh.shape["mp"]),
        mesh=mesh,
        in_specs=placed,
        out_specs=(P(None, ("mp", "dp"), None), P(None, "dp", "mp"), P(None, "dp", "mp", None)),
        check_vma=False,
    )
```
